512 devices in a mesh: mesh: 32 (over z, core), run: 16 (over y, x).
Axes of the slice: x: 4, y: 4, z: 16, core: 2. Of those that a mesh axis runs over, the one named last changes fastest.
Arguments:
- snapshots: bfloat16 [65536, 2048], P('mesh', 'run'), may hold values from -6 to 6
- block_cols: int32 [1024, 16], P('mesh'), may hold values from 0 to 1023, as said below
- mass_blocks: bfloat16 [1024, 64, 1024], P('mesh'), as said below
Outputs:
- gram: float32 [2048, 2048], P('mesh', 'run')
The draws below stay inside these ranges and needn't reach their ends.
Inputs may be any that keep to these rules, and one draw needn't show every extreme that they name: `block_cols`: block row b names 16 different block columns, the first of them b itself; all lie from 2 blocks before the first block row of shard b // 32 to 2 blocks after its last. In every shard but the first, its first block row names the block 2 before the shard; in every shard but the last, its last block row names the block 2 after it. `mass_blocks`: entry [b, i, k * 64 + j] is row i, column j of the k-th stored block of block row b, in the order of block_cols.
All inputs are finite; a program needn't handle non-finite values.
Results may differ from the reference program's by a relative error of at most 0.00056.
Values may be sent and summed in bfloat16 or wider, within the bound.
A program may use at most 64 MiB of HBM per device.

```python
import math
import jax
import jax.numpy as jnp
from jax import lax

SNAP = 2048
BLK = 64
KB = 16
HB = 2
NB = 32
NBLK = 1024
NODES = 65536
N_MESH = 32


def draw_block_cols(key, part):
    window_size = NB + 2 * HB
    position = jnp.arange(window_size, dtype=jnp.int32)[None, :]
    block_rows = jnp.arange(NBLK, dtype=jnp.int32)[:, None]
    shard_index = block_rows // NB
    inner_row = block_rows % NB
    global_cols = shard_index * NB - HB + position
    inside = (global_cols >= 0) & (global_cols < NBLK)
    random_score = jax.random.randint(key, (NBLK, window_size), 0, 2 ** 20, dtype=jnp.int32) * window_size + position
    forced_edge = (inner_row == 0) & (position == 0) | (inner_row == NB - 1) & (position == window_size - 1)
    scores = jnp.where(inside, random_score, -1 - position)
    scores = jnp.where(forced_edge & inside, 2 ** 29, scores)
    scores = jnp.where(position == inner_row + HB, 2 ** 30, scores)
    best_scores, chosen = lax.top_k(scores, KB)
    return (shard_index * NB - HB + chosen.astype(jnp.int32)).astype(jnp.int32)


def draw_mass_blocks(key, part):
    key_off = jax.random.fold_in(key, 11)
    key_diag = jax.random.fold_in(key, 23)
    off_blocks = jax.random.normal(key_off, (NBLK, KB, BLK, BLK), jnp.float32) * (0.5 / math.sqrt(KB * BLK))
    diagonal = jax.random.uniform(key_diag, (NBLK, BLK), jnp.float32, 0.5, 2.0)
    identity = jnp.eye(BLK, dtype=jnp.float32)
    first_slot = (jnp.arange(KB) == 0).astype(jnp.float32)
    assembled = off_blocks + first_slot[None, :, None, None] * identity[None, None] * diagonal[:, None, :, None]
    arranged = jnp.transpose(assembled, (0, 2, 1, 3)).reshape(NBLK, BLK, KB * BLK)
    return (arranged / NODES).astype(jnp.bfloat16)


def raised(entries, stream_key, source, target, parts, factor):
    owner, partner = [(jnp.arange(entries.shape[axis_at]) // (entries.shape[axis_at] // parts)).reshape([-1 if axis == axis_at else 1 for axis in range(entries.ndim)]) for axis_at in (source, target)]
    chosen = jax.random.permutation(stream_key, parts)[partner]
    strong = (owner == chosen) | (owner == (partner + parts // 2) % parts)
    return jnp.where(strong, factor * entries, entries)


def block_levels(rng, dims, cuts, low, top_value):
    def one(dim, blocks):
        steps = jax.random.uniform(jax.random.fold_in(jax.random.fold_in(rng, 6), dim), (blocks,), jnp.float32, low / len(cuts), top_value / len(cuts))
        return jnp.repeat(jnp.exp(steps), dims[dim] // blocks).reshape((-1,) + (1,) * (len(dims) - dim - 1))

    gain = one(*cuts[0])
    for cut in cuts[1:]:
        gain = gain * one(*cut)
    return gain


def noise_with(rng, extent, scale, most, cuts, heavy, held_as=jnp.bfloat16):
    entries = scale * jax.random.normal(rng, extent, jnp.float32)
    if cuts:
        entries = entries * block_levels(rng, extent, cuts, -0.22, 0.18)
    return jnp.clip(raised(entries, jax.random.fold_in(rng, 3), *heavy), -most, most).astype(held_as)


def setup_inputs(seed: int = 0) -> dict:
    seeds = jax.random.split(jax.random.key(seed), 4)
    snapshots = noise_with(seeds[0], (NODES, SNAP), 1.0, 6.0, ((0, 32), (1, 16)), (0, 1, 32, 2.75))
    block_cols = draw_block_cols(jax.random.fold_in(seeds[3], 71), 0)
    mass_blocks = draw_mass_blocks(jax.random.fold_in(seeds[3], 71), 0)
    return dict(snapshots=snapshots, block_cols=block_cols, mass_blocks=mass_blocks)


def reference(snapshots, block_cols, mass_blocks):
    block_total = block_cols.shape[0]
    blocked = snapshots.reshape(block_total, BLK, SNAP)

    def one_shard(pieces):
        shard_cols, shard_mass = pieces
        picked = blocked[shard_cols].reshape(NB, KB * BLK, SNAP)
        products = jnp.einsum("bim,bmc->bic", shard_mass.astype(jnp.float32), picked.astype(jnp.float32))
        return products.astype(jnp.bfloat16)

    weighted = lax.map(one_shard, (block_cols.reshape(N_MESH, NB, KB), mass_blocks.reshape(N_MESH, NB, BLK, KB * BLK)))
    weighted = weighted.reshape(NODES, SNAP)
    return lax.dot_general(snapshots, weighted, (((0,), (0,)), ((), ())), preferred_element_type=jnp.float32)
```

```python
import jax
import jax.numpy as jnp
from jax import lax
from jax.experimental import pallas as pl
from jax.experimental.pallas import tpu as pltpu
from jax.sharding import PartitionSpec as P

BLK = 64
HB = 2
MESH = pl.DeviceIdType.MESH
PARTS = 4


def kernel(
    snap_hbm, cols_hbm, mass_hbm, out_ref,
    cols, ext, sall, wall, mass, acc, comb, zsend, zrecv, red, fin,
    load_sem, halo_ss, halo_rs, s_ss, s_rs, w_ss, w_rs, c_ss, c_rs, z_ss, z_rs, f_ss, f_rs,
):
    m, r = lax.axis_index("mesh"), lax.axis_index("run")
    z, c, y, x = m // 2, m % 2, r // 4, r % 4
    kb, rows_b = cols.shape
    bpc = rows_b // PARTS

    def dev(z_, c_, y_, x_):
        return {"mesh": z_ * 2 + c_, "run": y_ * 4 + x_}

    y_up, y_dn = dev(z, c, (y + 1) % 4, x), dev(z, c, (y + 3) % 4, x)
    x_up, x_dn = dev(z, c, y, (x + 1) % 4), dev(z, c, y, (x + 3) % 4)
    m_up, m_dn = {"mesh": (m + 1) % 32, "run": r}, {"mesh": (m + 31) % 32, "run": r}
    sibling = dev(z, 1 - c, y, x)
    partner = dev((z // 4) * 4 + x, c, y, z % 4)
    moves = (z % 4) != x

    load_ext = pltpu.make_async_copy(snap_hbm, ext.at[pl.ds(HB, rows_b)], load_sem.at[0])
    load_own = pltpu.make_async_copy(snap_hbm, sall.at[y], load_sem.at[1])
    load_ext.start()
    load_own.start()
    load_cols = pltpu.make_async_copy(cols_hbm, cols, load_sem.at[2])
    load_cols.start()
    order = (0, 3, 1, 2)
    loads = {}
    for j in order:
        part = pl.ds(j * bpc, bpc)
        loads[j] = pltpu.make_async_copy(mass_hbm.at[part], mass.at[part], load_sem.at[3 + j])
        loads[j].start()

    barrier = pltpu.get_barrier_semaphore()
    for d in (y_up, y_dn, x_up, x_dn, m_up, m_dn):
        pl.semaphore_signal(barrier, inc=1, device_id=d, device_id_type=MESH)

    def greet(o, _):
        pl.semaphore_signal(barrier, inc=1, device_id=dev((z + o) % 16, c, y, x), device_id_type=MESH)
        return 0

    lax.fori_loop(1, 16, greet, 0)

    @pl.when(moves)
    def _():
        pl.semaphore_signal(barrier, inc=1, device_id=partner, device_id_type=MESH)

    pl.semaphore_wait(barrier, 21 + jnp.where(moves, 1, 0))

    def part_of(way, j):
        return j % PARTS if way == 0 else PARTS - 1 - j % PARTS

    def ring(buf, ss, rs, pos, up, dn, way, j, incoming=False):
        back = 3 if way == 0 else 1
        far = (j // PARTS) + (1 if incoming else 0)
        slot = (pos + back * far) % 4
        rows = pl.ds(part_of(way, j) * bpc, bpc)
        return pltpu.make_async_remote_copy(
            buf.at[slot, rows], buf.at[slot, rows], ss.at[way, j], rs.at[way, j],
            device_id=up if way == 0 else dn, device_id_type=MESH,
        )

    def s_copy(way, j, incoming=False):
        return ring(sall, s_ss, s_rs, y, y_up, y_dn, way, j, incoming)

    def w_copy(way, j, incoming=False):
        return ring(wall, w_ss, w_rs, x, x_up, x_dn, way, j, incoming)

    load_ext.wait()
    halo_up = pltpu.make_async_remote_copy(
        ext.at[pl.ds(rows_b, HB)], ext.at[pl.ds(0, HB)], halo_ss.at[0], halo_rs.at[0],
        device_id=m_up, device_id_type=MESH)
    halo_dn = pltpu.make_async_remote_copy(
        ext.at[pl.ds(HB, HB)], ext.at[pl.ds(rows_b + HB, HB)], halo_ss.at[1], halo_rs.at[1],
        device_id=m_dn, device_id_type=MESH)
    halo_up.start()
    halo_dn.start()
    load_own.wait()
    for j in range(PARTS):
        for way in (0, 1):
            s_copy(way, j).start()

    halo_up.wait_recv()
    halo_dn.wait_recv()
    load_cols.wait()
    base = m * rows_b - HB

    def weigh(b, _):
        picked = jnp.concatenate([ext[jnp.clip(cols[k, b] - base, 0, rows_b + 2 * HB - 1)] for k in range(kb)], axis=0)
        w = jnp.dot(mass[b], picked, preferred_element_type=jnp.float32)
        wall[x, b] = w.astype(jnp.bfloat16)
        return 0

    started = {0: 0, 1: 0}
    have = set()
    for j in order:
        loads[j].wait()
        lax.fori_loop(j * bpc, (j + 1) * bpc, weigh, 0, unroll=4)
        have.add(j)
        for way in (0, 1):
            while started[way] < PARTS and part_of(way, started[way]) in have:
                w_copy(way, started[way]).start()
                started[way] += 1

    for copy in (s_copy, w_copy):
        for j in range(PARTS // 2):
            for way in (0, 1):
                copy(way, j, True).wait_recv()
                copy(way, PARTS + j).start()

    for j in range(PARTS // 2, PARTS + PARTS // 2):
        for way in (0, 1):
            s_copy(way, j, True).wait_recv()

    def gram_part(slot, j, first):
        rows = pl.ds(j * bpc, bpc)
        left = jnp.concatenate([sall[q, rows].reshape(bpc * BLK, 128) for q in range(4)], axis=1)
        right = wall[slot, rows].reshape(bpc * BLK, 128)
        d = lax.dot_general(left, right, (((0,), (0,)), ((), ())), preferred_element_type=jnp.float32)
        d = d.reshape(4, 2, 64, 128)
        if first:
            acc[slot] = d
        else:
            acc[slot] += d

    def combine(slot):
        return pltpu.make_async_remote_copy(
            acc.at[slot, :, 1 - c], comb.at[slot], c_ss.at[slot], c_rs.at[slot],
            device_id=sibling, device_id_type=MESH)

    def z_copy(to, frm):
        return pltpu.make_async_remote_copy(
            zsend.at[to], zrecv.at[frm], z_ss.at[to], z_rs.at[frm],
            device_id=dev(to, c, y, x), device_id_type=MESH)

    def send_off(slot):
        combine(slot).wait_recv()

        def one(q, _):
            zsend[q * 4 + slot] = acc[slot, q, c] + comb[slot, q]

            @pl.when(q * 4 + slot != z)
            def _():
                z_copy(q * 4 + slot, z).start()
            return 0

        lax.fori_loop(0, 4, one, 0)

    slots = [x, (x + 3) % 4, (x + 1) % 4, (x + 2) % 4]
    for i, slot in enumerate(slots):
        if i in (1, 2):
            for j in range(PARTS // 2, PARTS):
                w_copy(i - 1, j, True).wait_recv()
        if i == 3:
            for j in range(PARTS, PARTS + PARTS // 2):
                for way in (0, 1):
                    w_copy(way, j, True).wait_recv()
        for j in range(PARTS):
            gram_part(slot, j, j == 0)
        combine(slot).start()
        if i > 0:
            send_off(slots[i - 1])
    send_off(slots[3])

    red[...] = zsend[z]

    def add(o, _):
        frm = (z + o) % 16
        z_copy(z, frm).wait_recv()
        red[...] += zrecv[frm]
        return 0

    lax.fori_loop(1, 16, add, 0)

    @pl.when(moves)
    def _():
        move = pltpu.make_async_remote_copy(red, fin, f_ss.at[0], f_rs.at[0], device_id=partner, device_id_type=MESH)
        move.start()
        move.wait()
        out_ref[...] = fin[...]

    @pl.when(jnp.logical_not(moves))
    def _():
        out_ref[...] = red[...]

    halo_up.wait_send()
    halo_dn.wait_send()
    for copy in (s_copy, w_copy):
        for j in range(PARTS + PARTS // 2):
            for way in (0, 1):
                copy(way, j).wait_send()
    for slot in range(4):
        combine(slot).wait_send()

    def drain(o, _):
        z_copy((z + o) % 16, z).wait_send()
        return 0

    lax.fori_loop(1, 16, drain, 0)


def on_device(snapshots, block_cols, mass_blocks):
    width = snapshots.shape[1]
    rows_b = block_cols.shape[0]
    snapshots = snapshots.reshape(rows_b, BLK, width)
    dma = pltpu.SemaphoreType.DMA
    steps = PARTS + PARTS // 2
    hbm = pl.BlockSpec(memory_space=pltpu.HBM)
    return pl.pallas_call(
        kernel,
        out_shape=jax.ShapeDtypeStruct((64, width), jnp.float32),
        in_specs=[hbm, hbm, hbm],
        out_specs=pl.BlockSpec(memory_space=pltpu.VMEM),
        scratch_shapes=[
            pltpu.SMEM(block_cols.shape[::-1], jnp.int32),
            pltpu.VMEM((rows_b + 2 * HB, BLK, width), jnp.bfloat16),
            pltpu.VMEM((4, rows_b, BLK, width), jnp.bfloat16),
            pltpu.VMEM((4, rows_b, BLK, width), jnp.bfloat16),
            pltpu.VMEM(mass_blocks.shape, jnp.bfloat16),
            pltpu.VMEM((4, 4, 2, 64, width), jnp.float32),
            pltpu.VMEM((4, 4, 64, width), jnp.float32),
            pltpu.VMEM((16, 64, width), jnp.float32),
            pltpu.VMEM((16, 64, width), jnp.float32),
            pltpu.VMEM((64, width), jnp.float32),
            pltpu.VMEM((64, width), jnp.float32),
            dma((3 + PARTS,)),
            dma((2,)), dma((2,)),
            dma((2, steps)), dma((2, steps)),
            dma((2, steps)), dma((2, steps)),
            dma((4,)), dma((4,)),
            dma((16,)), dma((16,)),
            dma((1,)), dma((1,)),
        ],
        compiler_params=pltpu.CompilerParams(
            collective_id=0, has_side_effects=True, vmem_limit_bytes=60 * 2**20),
        name="gram",
    )(snapshots, block_cols.T, mass_blocks)


def solution(mesh):
    placed = (P("mesh", "run"), P("mesh", None), P("mesh", None, None))
    return jax.shard_map(
        on_device, mesh=mesh, in_specs=placed, out_specs=P("mesh", "run"), check_vma=False
    )
```

```python
import jax
import jax.numpy as jnp
from jax import lax
from jax.experimental import pallas as pl
from jax.experimental.pallas import tpu as pltpu
from jax.sharding import PartitionSpec as P

BLK = 64
HB = 2
MESH = pl.DeviceIdType.MESH
PARTS = 4


def kernel(
    snap_hbm, cols_hbm, mass_hbm, out_ref,
    cols, ext, sall, wall, mass, acc, comb, zsend, merge, zrecv, red, fin,
    load_sem, halo_ss, halo_rs, s_ss, s_rs, w_ss, w_rs, c_ss, c_rs, m_ss, m_rs, z_ss, z_rs, f_ss, f_rs, relay,
):
    m, r = lax.axis_index("mesh"), lax.axis_index("run")
    z, c, y, x = m // 2, m % 2, r // 4, r % 4
    kb, rows_b = cols.shape
    bpc = rows_b // PARTS

    def dev(z_, c_, y_, x_):
        return {"mesh": z_ * 2 + c_, "run": y_ * 4 + x_}

    y_up, y_dn = dev(z, c, (y + 1) % 4, x), dev(z, c, (y + 3) % 4, x)
    x_up, x_dn = dev(z, c, y, (x + 1) % 4), dev(z, c, y, (x + 3) % 4)
    m_up, m_dn = {"mesh": (m + 1) % 32, "run": r}, {"mesh": (m + 31) % 32, "run": r}
    sibling = dev(z, 1 - c, y, x)
    z_up, z_dn = dev((z + 1) % 16, c, y, x), dev((z + 15) % 16, c, y, x)
    home = dev((z // 4) * 4 + x, c, y, (2 * x + 6 - z % 4) % 4)
    giver = dev((z // 4) * 4 + (2 * (z % 4) + 6 - x) % 4, c, y, z % 4)

    def greet(sem, devices):
        for d in devices:
            pl.semaphore_signal(sem, inc=1, device_id=d, device_id_type=MESH)

    load_ext = pltpu.make_async_copy(snap_hbm, ext.at[pl.ds(HB, rows_b)], load_sem.at[0])
    load_own = pltpu.make_async_copy(snap_hbm, sall.at[y], load_sem.at[1])
    load_ext.start()
    load_own.start()
    load_cols = pltpu.make_async_copy(cols_hbm, cols, load_sem.at[2])
    load_cols.start()
    order = (0, 3, 1, 2)
    loads = {}
    for j in order:
        part = pl.ds(j * bpc, bpc)
        loads[j] = pltpu.make_async_copy(mass_hbm.at[part], mass.at[part], load_sem.at[3 + j])
        loads[j].start()

    barrier = pltpu.get_barrier_semaphore()
    greet(barrier, (y_up, y_dn, x_up, x_dn, m_up, m_dn, z_up, z_dn, home, giver))
    pl.semaphore_wait(barrier, 10)
    greet(relay.at[0], (z_up, z_dn))

    def pass_on(i):
        pl.semaphore_wait(relay.at[i], 2)
        if i < 2:
            by = 2 ** (i + 1)
            greet(relay.at[i + 1], (dev((z + by) % 16, c, y, x), dev((z + 16 - by) % 16, c, y, x)))

    def part_of(way, j):
        return j % PARTS if way == 0 else PARTS - 1 - j % PARTS

    def ring(buf, ss, rs, pos, up, dn, way, j, incoming=False):
        back = 3 if way == 0 else 1
        far = (j // PARTS) + (1 if incoming else 0)
        slot = (pos + back * far) % 4
        rows = pl.ds(part_of(way, j) * bpc, bpc)
        return pltpu.make_async_remote_copy(
            buf.at[slot, rows], buf.at[slot, rows], ss.at[way, j], rs.at[way, j],
            device_id=up if way == 0 else dn, device_id_type=MESH,
        )

    def s_copy(way, j, incoming=False):
        return ring(sall, s_ss, s_rs, y, y_up, y_dn, way, j, incoming)

    def w_copy(way, j, incoming=False):
        return ring(wall, w_ss, w_rs, x, x_up, x_dn, way, j, incoming)

    load_ext.wait()
    halo_up = pltpu.make_async_remote_copy(
        ext.at[pl.ds(rows_b, HB)], ext.at[pl.ds(0, HB)], halo_ss.at[0], halo_rs.at[0],
        device_id=m_up, device_id_type=MESH)
    halo_dn = pltpu.make_async_remote_copy(
        ext.at[pl.ds(HB, HB)], ext.at[pl.ds(rows_b + HB, HB)], halo_ss.at[1], halo_rs.at[1],
        device_id=m_dn, device_id_type=MESH)
    halo_up.start()
    halo_dn.start()
    load_own.wait()
    for j in range(PARTS):
        for way in (0, 1):
            s_copy(way, j).start()

    halo_up.wait_recv()
    halo_dn.wait_recv()
    pass_on(0)
    load_cols.wait()
    base = m * rows_b - HB

    def weigh(b, _):
        picked = jnp.concatenate([ext[jnp.clip(cols[k, b] - base, 0, rows_b + 2 * HB - 1)] for k in range(kb)], axis=0)
        w = jnp.dot(mass[b], picked, preferred_element_type=jnp.float32)
        wall[x, b] = w.astype(jnp.bfloat16)
        return 0

    started = {0: 0, 1: 0}
    have = set()
    for j in order:
        loads[j].wait()
        lax.fori_loop(j * bpc, (j + 1) * bpc, weigh, 0, unroll=4)
        have.add(j)
        for way in (0, 1):
            while started[way] < PARTS and part_of(way, started[way]) in have:
                w_copy(way, started[way]).start()
                started[way] += 1

    for copy in (s_copy, w_copy):
        for j in range(PARTS // 2):
            for way in (0, 1):
                copy(way, j, True).wait_recv()
                copy(way, PARTS + j).start()
    pass_on(1)

    def left(ps, j):
        rows = pl.ds(j * bpc, bpc)
        return jnp.concatenate([sall[(y + p + 3) % 4, rows].reshape(bpc * BLK, 128) for p in ps], axis=1)

    def right(ps, j):
        rows = pl.ds(j * bpc, bpc)
        return jnp.concatenate([wall[(x + p + 3) % 4, rows].reshape(bpc * BLK, 128) for p in ps], axis=1)

    def gram_part(ws, ss, j, first):
        d = lax.dot_general(left(ss, j), right(ws, j), (((0,), (0,)), ((), ())), preferred_element_type=jnp.float32)
        for iw, w in enumerate(ws):
            for i_s, s in enumerate(ss):
                t = d[128 * i_s:128 * (i_s + 1), 128 * iw:128 * (iw + 1)].reshape(2, 64, 128)
                if first:
                    acc[w, s] = t
                else:
                    acc[w, s] += t

    near, far = (0, 1, 2), (3,)
    three = pl.ds(0, 3)
    groups = (
        (9, lambda n: n // 3, lambda n: n % 3, (three, three)),
        (3, lambda n: n, lambda n: 3, (three, 3)),
        (4, lambda n: 3, lambda n: n, (3, pl.ds(0, 4))),
    )

    def combine(g):
        w, s = groups[g][3]
        return pltpu.make_async_remote_copy(
            acc.at[w, s, 1 - c], comb.at[w, s], c_ss.at[g], c_rs.at[g], device_id=sibling, device_id_type=MESH)

    def m_copy(d, o):
        return pltpu.make_async_remote_copy(
            zsend.at[d], merge.at[d], m_ss.at[d], m_rs.at[d],
            device_id=dev((z + jnp.where(o <= 8, 1, 15)) % 16, c, y, x), device_id_type=MESH)

    def z_copy(to, frm):
        return pltpu.make_async_remote_copy(
            zsend.at[to], zrecv.at[frm], z_ss.at[to], z_rs.at[frm], device_id=dev(to, c, y, x), device_id_type=MESH)

    def chip(w, s):
        d = ((y + s + 3) % 4) * 4 + (x + 7 - w) % 4
        return d, (d - z + 16) % 16

    def send_next(g):
        count, w_of, s_of, _ = groups[g]
        combine(g).wait_recv()

        def one(n, _):
            w, s = w_of(n), s_of(n)
            d, o = chip(w, s)
            zsend[d] = acc[w, s, c] + comb[w, s]

            @pl.when((o % 2 == 0) & (o != 0))
            def _():
                m_copy(d, o).start()
            return 0

        lax.fori_loop(0, count, one, 0)

    def send_far(g):
        count, w_of, s_of, _ = groups[g]

        def one(n, _):
            d, o = chip(w_of(n), s_of(n))

            @pl.when(o % 2 == 1)
            def _():
                @pl.when(o != 9)
                def _():
                    m_copy(d, o).wait_recv()
                    zsend[d] += merge[d]
                z_copy(d, z).start()
            return 0

        lax.fori_loop(0, count, one, 0)

    for j in range(PARTS // 2, PARTS):
        for way in (0, 1):
            s_copy(way, j, True).wait_recv()
            w_copy(way, j, True).wait_recv()
    for j in range(PARTS):
        gram_part(near, near, j, j == 0)
    combine(0).start()
    for j in range(PARTS, PARTS + PARTS // 2):
        for way in (0, 1):
            s_copy(way, j, True).wait_recv()
    for j in range(PARTS):
        gram_part(near, far, j, j == 0)
    combine(1).start()
    send_next(0)
    send_next(1)
    pass_on(2)
    send_far(0)
    send_far(1)
    for j in range(PARTS, PARTS + PARTS // 2):
        for way in (0, 1):
            w_copy(way, j, True).wait_recv()
            gram_part(far, near + far, part_of(way, j), j == PARTS and way == 0)
    combine(2).start()
    send_next(2)
    send_far(2)

    red[...] = zsend[z]

    def add(n, _):
        frm = (z + 1 + 2 * n) % 16
        z_copy(z, frm).wait_recv()
        red[...] += zrecv[frm]
        return 0

    lax.fori_loop(0, 8, add, 0)
    move = pltpu.make_async_remote_copy(red, fin, f_ss.at[0], f_rs.at[0], device_id=home, device_id_type=MESH)
    move.start()
    move.wait()
    out_ref[...] = fin[...]

    halo_up.wait_send()
    halo_dn.wait_send()
    for copy in (s_copy, w_copy):
        for j in range(PARTS + PARTS // 2):
            for way in (0, 1):
                copy(way, j).wait_send()
    for g in range(3):
        combine(g).wait_send()

    def drain(o, _):
        d = (z + o) % 16

        @pl.when(o % 2 == 0)
        def _():
            m_copy(d, o).wait_send()

        @pl.when(o % 2 == 1)
        def _():
            z_copy(d, z).wait_send()
        return 0

    lax.fori_loop(1, 16, drain, 0)


def on_device(snapshots, block_cols, mass_blocks):
    width = snapshots.shape[1]
    rows_b = block_cols.shape[0]
    snapshots = snapshots.reshape(rows_b, BLK, width)
    dma = pltpu.SemaphoreType.DMA
    steps = PARTS + PARTS // 2
    hbm = pl.BlockSpec(memory_space=pltpu.HBM)
    return pl.pallas_call(
        kernel,
        out_shape=jax.ShapeDtypeStruct((64, width), jnp.float32),
        in_specs=[hbm, hbm, hbm],
        out_specs=pl.BlockSpec(memory_space=pltpu.VMEM),
        scratch_shapes=[
            pltpu.SMEM(block_cols.shape[::-1], jnp.int32),
            pltpu.VMEM((rows_b + 2 * HB, BLK, width), jnp.bfloat16),
            pltpu.VMEM((4, rows_b, BLK, width), jnp.bfloat16),
            pltpu.VMEM((4, rows_b, BLK, width), jnp.bfloat16),
            pltpu.VMEM(mass_blocks.shape, jnp.bfloat16),
            pltpu.VMEM((4, 4, 2, 64, width), jnp.float32),
            pltpu.VMEM((4, 4, 64, width), jnp.float32),
            pltpu.VMEM((16, 64, width), jnp.float32),
            pltpu.VMEM((16, 64, width), jnp.float32),
            pltpu.VMEM((16, 64, width), jnp.float32),
            pltpu.VMEM((64, width), jnp.float32),
            pltpu.VMEM((64, width), jnp.float32),
            dma((3 + PARTS,)),
            dma((2,)), dma((2,)),
            dma((2, steps)), dma((2, steps)),
            dma((2, steps)), dma((2, steps)),
            dma((3,)), dma((3,)),
            dma((16,)), dma((16,)),
            dma((16,)), dma((16,)),
            dma((1,)), dma((1,)),
            pltpu.SemaphoreType.REGULAR((3,)),
        ],
        compiler_params=pltpu.CompilerParams(
            collective_id=0, has_side_effects=True, vmem_limit_bytes=60 * 2**20),
        name="gram",
    )(snapshots, block_cols.T, mass_blocks)


def solution(mesh):
    placed = (P("mesh", "run"), P("mesh", None), P("mesh", None, None))
    return jax.shard_map(
        on_device, mesh=mesh, in_specs=placed, out_specs=P("mesh", "run"), check_vma=False
    )
```

```python
import jax
import jax.numpy as jnp
from jax import lax
from jax.experimental import pallas as pl
from jax.experimental.pallas import tpu as pltpu
from jax.sharding import PartitionSpec as P

BLK = 64
HB = 2
MESH = pl.DeviceIdType.MESH
PARTS = 4


SENT = 33
CODE = 32000.0


def code(v):
    power = jnp.ceil(jnp.log2(jnp.maximum(jnp.max(jnp.abs(v), axis=0, keepdims=True), 1e-30)))
    q = jnp.round(v * (jnp.exp2(-power) * CODE)).astype(jnp.int32)
    half = v.shape[0] // 2
    return (q[:half] << 16) | (q[half:] & 0xFFFF), power.astype(jnp.int32)


def decode(pairs, power):
    q = jnp.concatenate([pairs >> 16, (pairs << 16) >> 16], axis=0)
    return q.astype(jnp.float32) * (jnp.exp2(power.astype(jnp.float32)) * (1 / CODE))


def kernel(
    snap_hbm, cols_hbm, mass_hbm, out_ref,
    cols, ext, sall, wall, mass, acc, comb, share, zsend, merge, zrecv, red, fin,
    load_sem, halo_ss, halo_rs, s_ss, s_rs, w_ss, w_rs, c_ss, c_rs, m_ss, m_rs, z_ss, z_rs, f_ss, f_rs, relay,
):
    m, r = lax.axis_index("mesh"), lax.axis_index("run")
    z, c, y, x = m // 2, m % 2, r // 4, r % 4
    kb, rows_b = cols.shape
    bpc = rows_b // PARTS

    def dev(z_, c_, y_, x_):
        return {"mesh": z_ * 2 + c_, "run": y_ * 4 + x_}

    y_up, y_dn = dev(z, c, (y + 1) % 4, x), dev(z, c, (y + 3) % 4, x)
    x_up, x_dn = dev(z, c, y, (x + 1) % 4), dev(z, c, y, (x + 3) % 4)
    m_up, m_dn = {"mesh": (m + 1) % 32, "run": r}, {"mesh": (m + 31) % 32, "run": r}
    sibling = dev(z, 1 - c, y, x)
    z_up, z_dn = dev((z + 1) % 16, c, y, x), dev((z + 15) % 16, c, y, x)
    home = dev((z // 4) * 4 + x, c, y, (2 * x + 6 - z % 4) % 4)
    giver = dev((z // 4) * 4 + (2 * (z % 4) + 6 - x) % 4, c, y, z % 4)

    def greet(sem, devices):
        for d in devices:
            pl.semaphore_signal(sem, inc=1, device_id=d, device_id_type=MESH)

    load_ext = pltpu.make_async_copy(snap_hbm, ext.at[pl.ds(HB, rows_b)], load_sem.at[0])
    load_own = pltpu.make_async_copy(snap_hbm, sall.at[y], load_sem.at[1])
    load_ext.start()
    load_own.start()
    load_cols = pltpu.make_async_copy(cols_hbm, cols, load_sem.at[2])
    load_cols.start()
    order = (0, 3, 1, 2)
    loads = {}
    for j in order:
        part = pl.ds(j * bpc, bpc)
        loads[j] = pltpu.make_async_copy(mass_hbm.at[part], mass.at[part], load_sem.at[3 + j])
        loads[j].start()

    barrier = pltpu.get_barrier_semaphore()
    greet(barrier, (y_up, y_dn, x_up, x_dn, m_up, m_dn, z_up, z_dn, home, giver))
    pl.semaphore_wait(barrier, 10)
    greet(relay.at[0], (z_up, z_dn))

    def pass_on(i):
        pl.semaphore_wait(relay.at[i], 2)
        if i < 2:
            by = 2 ** (i + 1)
            greet(relay.at[i + 1], (dev((z + by) % 16, c, y, x), dev((z + 16 - by) % 16, c, y, x)))

    def part_of(way, j):
        return j % PARTS if way == 0 else PARTS - 1 - j % PARTS

    def ring(buf, ss, rs, pos, up, dn, way, j, incoming=False):
        back = 3 if way == 0 else 1
        far = (j // PARTS) + (1 if incoming else 0)
        slot = (pos + back * far) % 4
        rows = pl.ds(part_of(way, j) * bpc, bpc)
        return pltpu.make_async_remote_copy(
            buf.at[slot, rows], buf.at[slot, rows], ss.at[way, j], rs.at[way, j],
            device_id=up if way == 0 else dn, device_id_type=MESH,
        )

    def s_copy(way, j, incoming=False):
        return ring(sall, s_ss, s_rs, y, y_up, y_dn, way, j, incoming)

    def w_copy(way, j, incoming=False):
        return ring(wall, w_ss, w_rs, x, x_up, x_dn, way, j, incoming)

    load_ext.wait()
    halo_up = pltpu.make_async_remote_copy(
        ext.at[pl.ds(rows_b, HB)], ext.at[pl.ds(0, HB)], halo_ss.at[0], halo_rs.at[0],
        device_id=m_up, device_id_type=MESH)
    halo_dn = pltpu.make_async_remote_copy(
        ext.at[pl.ds(HB, HB)], ext.at[pl.ds(rows_b + HB, HB)], halo_ss.at[1], halo_rs.at[1],
        device_id=m_dn, device_id_type=MESH)
    halo_up.start()
    halo_dn.start()
    load_own.wait()
    for j in range(PARTS):
        for way in (0, 1):
            s_copy(way, j).start()

    halo_up.wait_recv()
    halo_dn.wait_recv()
    pass_on(0)
    load_cols.wait()
    base = m * rows_b - HB

    def weigh(b, _):
        picked = jnp.concatenate([ext[jnp.clip(cols[k, b] - base, 0, rows_b + 2 * HB - 1)] for k in range(kb)], axis=0)
        w = jnp.dot(mass[b], picked, preferred_element_type=jnp.float32)
        wall[x, b] = w.astype(jnp.bfloat16)
        return 0

    started = {0: 0, 1: 0}
    have = set()
    for j in order:
        loads[j].wait()
        lax.fori_loop(j * bpc, (j + 1) * bpc, weigh, 0, unroll=4)
        have.add(j)
        for way in (0, 1):
            while started[way] < PARTS and part_of(way, started[way]) in have:
                w_copy(way, started[way]).start()
                started[way] += 1

    for copy in (s_copy, w_copy):
        for j in range(PARTS // 2):
            for way in (0, 1):
                copy(way, j, True).wait_recv()
                copy(way, PARTS + j).start()
    pass_on(1)

    def along_x(p):
        return p + p // 2 - 2 * (p // 3)

    def left(ps, j):
        rows = pl.ds(j * bpc, bpc)
        return jnp.concatenate([sall[(y + p + 3) % 4, rows].reshape(bpc * BLK, 128) for p in ps], axis=1)

    def right(ps, j):
        rows = pl.ds(j * bpc, bpc)
        return jnp.concatenate([wall[(x + along_x(p)) % 4, rows].reshape(bpc * BLK, 128) for p in ps], axis=1)

    def gram_part(ws, ss, j, first):
        d = lax.dot_general(left(ss, j), right(ws, j), (((0,), (0,)), ((), ())), preferred_element_type=jnp.float32)
        for iw, w in enumerate(ws):
            for i_s, s in enumerate(ss):
                t = d[128 * i_s:128 * (i_s + 1), 128 * iw:128 * (iw + 1)].reshape(2, 64, 128)
                if first:
                    acc[w, s] = t
                else:
                    acc[w, s] += t

    own, beside, near, far = (0,), (1, 2), (0, 1, 2), (3,)
    three = pl.ds(0, 3)
    groups = (
        (3, lambda n: 0, lambda n: n, (0, three)),
        (6, lambda n: 1 + n // 3, lambda n: n % 3, (pl.ds(1, 2), three)),
        (3, lambda n: n, lambda n: 3, (three, 3)),
        (4, lambda n: 3, lambda n: n, (3, pl.ds(0, 4))),
    )

    def combine(g):
        w, s = groups[g][3]
        return pltpu.make_async_remote_copy(
            acc.at[w, s, 1 - c], comb.at[w, s], c_ss.at[g], c_rs.at[g], device_id=sibling, device_id_type=MESH)

    sent = pl.ds(0, SENT)

    def put(d, v):
        pairs, power = code(v)
        zsend[d, 0:32] = pairs
        zsend[d, 32:40] = jnp.broadcast_to(power, (8, power.shape[1]))

    def taken(ref, i):
        return decode(ref[i, 0:32], ref[i, 32:33])

    def m_copy(d, o):
        return pltpu.make_async_remote_copy(
            zsend.at[d, sent], merge.at[d, sent], m_ss.at[d], m_rs.at[d],
            device_id=dev((z + jnp.where(o <= 8, 1, 15)) % 16, c, y, x), device_id_type=MESH)

    def z_copy(to, frm):
        return pltpu.make_async_remote_copy(
            zsend.at[to, sent], zrecv.at[frm, sent], z_ss.at[to], z_rs.at[frm], device_id=dev(to, c, y, x), device_id_type=MESH)

    def chip(w, s):
        d = ((y + s + 3) % 4) * 4 + (x + 6 - along_x(w)) % 4
        return d, (d - z + 16) % 16

    def send_next(g):
        count, w_of, s_of, _ = groups[g]
        combine(g).wait_recv()

        def one(n, _):
            w, s = w_of(n), s_of(n)
            d, o = chip(w, s)
            share[d] = acc[w, s, c] + comb[w, s]

            @pl.when((o % 2 == 0) & (o != 0))
            def _():
                put(d, share[d])
                m_copy(d, o).start()
            return 0

        lax.fori_loop(0, count, one, 0)

    def send_far(g):
        count, w_of, s_of, _ = groups[g]

        def one(n, _):
            d, o = chip(w_of(n), s_of(n))

            @pl.when(o % 2 == 1)
            def _():
                @pl.when(o != 9)
                def _():
                    m_copy(d, o).wait_recv()
                    share[d] += taken(merge, d)
                put(d, share[d])
                z_copy(d, z).start()
            return 0

        lax.fori_loop(0, count, one, 0)

    def arrived(copy, first, last):
        for j in range(first, last):
            for way in (0, 1):
                copy(way, j, True).wait_recv()

    def gram(ws, ss):
        for j in range(PARTS):
            gram_part(ws, ss, j, j == 0)

    arrived(s_copy, PARTS // 2, PARTS)
    gram(own, near)
    combine(0).start()
    send_next(0)
    arrived(w_copy, PARTS // 2, PARTS)
    gram(beside, near)
    combine(1).start()
    pass_on(2)
    send_far(0)
    send_next(1)
    arrived(s_copy, PARTS, PARTS + PARTS // 2)
    gram(near, far)
    combine(2).start()
    send_next(2)
    send_far(1)
    for j in range(PARTS, PARTS + PARTS // 2):
        for way in (0, 1):
            w_copy(way, j, True).wait_recv()
            gram_part(far, near + far, part_of(way, j), j == PARTS and way == 0)
    combine(3).start()
    send_far(2)
    send_next(3)
    send_far(3)

    red[...] = share[z]

    def add(n, _):
        frm = (z + 1 + 2 * n) % 16
        z_copy(z, frm).wait_recv()
        red[...] += taken(zrecv, frm)
        return 0

    lax.fori_loop(0, 8, add, 0)
    move = pltpu.make_async_remote_copy(red, fin, f_ss.at[0], f_rs.at[0], device_id=home, device_id_type=MESH)
    move.start()
    move.wait()
    out_ref[...] = fin[...]

    halo_up.wait_send()
    halo_dn.wait_send()
    for copy in (s_copy, w_copy):
        for j in range(PARTS + PARTS // 2):
            for way in (0, 1):
                copy(way, j).wait_send()
    for g in range(4):
        combine(g).wait_send()

    def drain(o, _):
        d = (z + o) % 16

        @pl.when(o % 2 == 0)
        def _():
            m_copy(d, o).wait_send()

        @pl.when(o % 2 == 1)
        def _():
            z_copy(d, z).wait_send()
        return 0

    lax.fori_loop(1, 16, drain, 0)


def on_device(snapshots, block_cols, mass_blocks):
    width = snapshots.shape[1]
    rows_b = block_cols.shape[0]
    snapshots = snapshots.reshape(rows_b, BLK, width)
    dma = pltpu.SemaphoreType.DMA
    steps = PARTS + PARTS // 2
    hbm = pl.BlockSpec(memory_space=pltpu.HBM)
    return pl.pallas_call(
        kernel,
        out_shape=jax.ShapeDtypeStruct((64, width), jnp.float32),
        in_specs=[hbm, hbm, hbm],
        out_specs=pl.BlockSpec(memory_space=pltpu.VMEM),
        scratch_shapes=[
            pltpu.SMEM(block_cols.shape[::-1], jnp.int32),
            pltpu.VMEM((rows_b + 2 * HB, BLK, width), jnp.bfloat16),
            pltpu.VMEM((4, rows_b, BLK, width), jnp.bfloat16),
            pltpu.VMEM((4, rows_b, BLK, width), jnp.bfloat16),
            pltpu.VMEM(mass_blocks.shape, jnp.bfloat16),
            pltpu.VMEM((4, 4, 2, 64, width), jnp.float32),
            pltpu.VMEM((4, 4, 64, width), jnp.float32),
            pltpu.VMEM((16, 64, width), jnp.float32),
            pltpu.VMEM((16, 40, width), jnp.int32),
            pltpu.VMEM((16, 40, width), jnp.int32),
            pltpu.VMEM((16, 40, width), jnp.int32),
            pltpu.VMEM((64, width), jnp.float32),
            pltpu.VMEM((64, width), jnp.float32),
            dma((3 + PARTS,)),
            dma((2,)), dma((2,)),
            dma((2, steps)), dma((2, steps)),
            dma((2, steps)), dma((2, steps)),
            dma((4,)), dma((4,)),
            dma((16,)), dma((16,)),
            dma((16,)), dma((16,)),
            dma((1,)), dma((1,)),
            pltpu.SemaphoreType.REGULAR((3,)),
        ],
        compiler_params=pltpu.CompilerParams(
            collective_id=0, has_side_effects=True, vmem_limit_bytes=60 * 2**20),
        name="gram",
    )(snapshots, block_cols.T, mass_blocks)


def solution(mesh):
    placed = (P("mesh", "run"), P("mesh", None), P("mesh", None, None))
    return jax.shard_map(
        on_device, mesh=mesh, in_specs=placed, out_specs=P("mesh", "run"), check_vma=False
    )
```

```python
import jax
import jax.numpy as jnp
from jax import lax
from jax.experimental import pallas as pl
from jax.experimental.pallas import tpu as pltpu
from jax.sharding import PartitionSpec as P

BLK = 64
HB = 2
MESH = pl.DeviceIdType.MESH
PARTS = 4


SENT = 33
CODE = 32000.0


def code(v):
    power = jnp.ceil(jnp.log2(jnp.maximum(jnp.max(jnp.abs(v), axis=1, keepdims=True), 1e-30)))
    q = jnp.round(v * (jnp.exp2(-power) * CODE)).astype(jnp.int32)
    half = v.shape[1] // 2
    return (q[:, :half] << 16) | (q[:, half:] & 0xFFFF), power.astype(jnp.int32)


def decode(pairs, power):
    q = jnp.concatenate([pairs >> 16, (pairs << 16) >> 16], axis=1)
    return q.astype(jnp.float32) * (jnp.exp2(power.astype(jnp.float32)) * (1 / CODE))


def kernel(
    snap_hbm, cols_hbm, mass_hbm, out_ref,
    cols, ext, sall, wall, mass, acc, comb, share, coded, zrecv, red, fin,
    load_sem, halo_ss, halo_rs, s_ss, s_rs, w_ss, w_rs, c_ss, c_rs, z_ss, z_rs, f_ss, f_rs, relay,
):
    m, r = lax.axis_index("mesh"), lax.axis_index("run")
    z, c, y, x = m // 2, m % 2, r // 4, r % 4
    kb, rows_b = cols.shape
    bpc = rows_b // PARTS

    def dev(z_, c_, y_, x_):
        return {"mesh": z_ * 2 + c_, "run": y_ * 4 + x_}

    y_up, y_dn = dev(z, c, (y + 1) % 4, x), dev(z, c, (y + 3) % 4, x)
    x_up, x_dn = dev(z, c, y, (x + 1) % 4), dev(z, c, y, (x + 3) % 4)
    m_up, m_dn = {"mesh": (m + 1) % 32, "run": r}, {"mesh": (m + 31) % 32, "run": r}
    sibling = dev(z, 1 - c, y, x)
    z_up, z_dn = dev((z + 1) % 16, c, y, x), dev((z + 15) % 16, c, y, x)
    home = dev((z // 4) * 4 + x, c, y, (2 * x + 6 - z % 4) % 4)
    giver = dev((z // 4) * 4 + (2 * (z % 4) + 6 - x) % 4, c, y, z % 4)

    def greet(sem, devices):
        for d in devices:
            pl.semaphore_signal(sem, inc=1, device_id=d, device_id_type=MESH)

    barrier = pltpu.get_barrier_semaphore()
    greet(barrier, (y_up, y_dn, x_up, x_dn, m_up, m_dn, z_up, z_dn))

    load_ext = pltpu.make_async_copy(snap_hbm, ext.at[pl.ds(HB, rows_b)], load_sem.at[0])
    load_own = pltpu.make_async_copy(snap_hbm, sall.at[y], load_sem.at[1])
    load_ext.start()
    load_own.start()
    load_cols = pltpu.make_async_copy(cols_hbm, cols, load_sem.at[2])
    load_cols.start()
    order = (0, 3, 1, 2)
    loads = {}
    for j in order:
        part = pl.ds(j * bpc, bpc)
        loads[j] = pltpu.make_async_copy(mass_hbm.at[part], mass.at[part], load_sem.at[3 + j])
        loads[j].start()

    pl.semaphore_wait(barrier, 8)
    greet(relay.at[0], (z_up, z_dn, x_up, x_dn, sibling))

    def pass_on(i):
        pl.semaphore_wait(relay.at[i], 5 if i == 0 else 2)
        if i < 2:
            by = 2 ** (i + 1)
            greet(relay.at[i + 1], (dev((z + by) % 16, c, y, x), dev((z + 16 - by) % 16, c, y, x)))

    def part_of(way, j):
        return j % PARTS if way == 0 else PARTS - 1 - j % PARTS

    def ring(buf, ss, rs, pos, up, dn, way, j, incoming=False):
        back = 3 if way == 0 else 1
        far = (j // PARTS) + (1 if incoming else 0)
        slot = (pos + back * far) % 4
        rows = pl.ds(part_of(way, j) * bpc, bpc)
        return pltpu.make_async_remote_copy(
            buf.at[slot, rows], buf.at[slot, rows], ss.at[way, j], rs.at[way, j],
            device_id=up if way == 0 else dn, device_id_type=MESH,
        )

    def s_copy(way, j, incoming=False):
        return ring(sall, s_ss, s_rs, y, y_up, y_dn, way, j, incoming)

    def w_copy(way, j, incoming=False):
        return ring(wall, w_ss, w_rs, x, x_up, x_dn, way, j, incoming)

    load_ext.wait()
    halo_up = pltpu.make_async_remote_copy(
        ext.at[pl.ds(rows_b, HB)], ext.at[pl.ds(0, HB)], halo_ss.at[0], halo_rs.at[0],
        device_id=m_up, device_id_type=MESH)
    halo_dn = pltpu.make_async_remote_copy(
        ext.at[pl.ds(HB, HB)], ext.at[pl.ds(rows_b + HB, HB)], halo_ss.at[1], halo_rs.at[1],
        device_id=m_dn, device_id_type=MESH)
    halo_up.start()
    halo_dn.start()
    load_own.wait()
    for j in range(PARTS):
        for way in (0, 1):
            s_copy(way, j).start()

    halo_up.wait_recv()
    halo_dn.wait_recv()
    pass_on(0)
    load_cols.wait()
    base = m * rows_b - HB

    def weigh(b, _):
        picked = jnp.concatenate([ext[jnp.clip(cols[k, b] - base, 0, rows_b + 2 * HB - 1)] for k in range(kb)], axis=0)
        w = jnp.dot(mass[b], picked, preferred_element_type=jnp.float32)
        wall[x, b] = w.astype(jnp.bfloat16)
        return 0

    started = {0: 0, 1: 0}
    have = set()
    for j in order:
        loads[j].wait()
        lax.fori_loop(j * bpc, (j + 1) * bpc, weigh, 0, unroll=4)
        have.add(j)
        for way in (0, 1):
            while started[way] < PARTS and part_of(way, started[way]) in have:
                w_copy(way, started[way]).start()
                started[way] += 1

    for copy in (s_copy, w_copy):
        for j in range(PARTS // 2):
            for way in (0, 1):
                copy(way, j, True).wait_recv()
                copy(way, PARTS + j).start()
        if copy is s_copy:
            pass_on(1)

    def along_x(p):
        return p + p // 2 - 2 * (p // 3)

    def left(ps, j):
        rows = pl.ds(j * bpc, bpc)
        return jnp.concatenate([sall[(y + p + 3) % 4, rows].reshape(bpc * BLK, 128) for p in ps], axis=1)

    def right(ps, j):
        rows = pl.ds(j * bpc, bpc)
        return jnp.concatenate([wall[(x + along_x(p)) % 4, rows].reshape(bpc * BLK, 128) for p in ps], axis=1)

    def gram_part(ws, ss, j, first):
        d = lax.dot_general(left(ss, j), right(ws, j), (((0,), (0,)), ((), ())), preferred_element_type=jnp.float32)
        for iw, w in enumerate(ws):
            for i_s, s in enumerate(ss):
                t = d[128 * i_s:128 * (i_s + 1), 128 * iw:128 * (iw + 1)].reshape(2, 64, 128)
                if first:
                    acc[w, s] = t
                else:
                    acc[w, s] += t

    own, beside, near, far = (0,), (1, 2), (0, 1, 2), (3,)
    three = pl.ds(0, 3)
    groups = (
        (3, lambda n: 0, lambda n: n, (0, three)),
        (6, lambda n: 1 + n // 3, lambda n: n % 3, (pl.ds(1, 2), three)),
        (3, lambda n: n, lambda n: 3, (three, 3)),
        (4, lambda n: 3, lambda n: n, (3, pl.ds(0, 4))),
    )

    def combine(g):
        w, s = groups[g][3]
        return pltpu.make_async_remote_copy(
            acc.at[w, s, 1 - c], comb.at[w, s], c_ss.at[g], c_rs.at[g], device_id=sibling, device_id_type=MESH)

    sent = pl.ds(0, SENT)

    def put(ref, v, *at):
        pairs, power = code(v.reshape(-1, *v.shape[-2:]))
        lead = v.shape[:-2]
        ref[*at, 0:32] = pairs.reshape(*lead, *pairs.shape[1:])
        ref[*at, 32:40] = jnp.broadcast_to(power, (power.shape[0], 8, power.shape[2])).reshape(*lead, 8, power.shape[2])

    def taken(ref, *at):
        pairs, power = ref[*at, 0:32], ref[*at, 32:33]
        lead = pairs.shape[:-2]
        v = decode(pairs.reshape(-1, *pairs.shape[-2:]), power.reshape(-1, *power.shape[-2:]))
        return v.reshape(*lead, *v.shape[1:])

    def z_copy(w, s, to, frm):
        return pltpu.make_async_remote_copy(
            coded.at[w, s, sent], zrecv.at[frm, sent], z_ss.at[w, s], z_rs.at[frm],
            device_id=dev(to, c, y, x), device_id_type=MESH)

    def chip(w, s):
        d = ((y + s + 3) % 4) * 4 + (x + 6 - along_x(w)) % 4
        return d, (d - z + 16) % 16

    def each(g, body):
        def one(n, _):
            w, s = groups[g][1](n), groups[g][2](n)
            body(w, s, *chip(w, s))
            return 0

        lax.fori_loop(0, groups[g][0], one, 0)

    def send(g):
        at = groups[g][3]
        combine(g).wait_recv()
        share[*at] = acc[*at, c] + comb[*at]
        put(coded, share[*at], *at)

        def one(w, s, d, o):
            @pl.when(o != 0)
            def _():
                z_copy(w, s, d, z).start()

        each(g, one)

    def arrived(copy, first, last):
        for j in range(first, last):
            for way in (0, 1):
                copy(way, j, True).wait_recv()

    def gram(ws, ss):
        for j in range(PARTS):
            gram_part(ws, ss, j, j == 0)

    arrived(s_copy, PARTS // 2, PARTS)
    gram(own, near)
    combine(0).start()
    pass_on(2)
    send(0)
    arrived(w_copy, PARTS // 2, PARTS)
    gram(beside, near)
    combine(1).start()
    arrived(s_copy, PARTS, PARTS + PARTS // 2)
    gram(near, far)
    combine(2).start()
    send(1)
    send(2)
    for j in range(PARTS, PARTS + PARTS // 2):
        for way in (0, 1):
            w_copy(way, j, True).wait_recv()
            gram_part(far, near + far, part_of(way, j), j == PARTS and way == 0)
    combine(3).start()
    send(3)

    red[...] = share[along_x((x + 6 - z % 4) % 4), (z // 4 - y + 5) % 4]

    def add(n, _):
        by = n // 2 + 1
        frm = (z + by + (n % 2) * (16 - 2 * by)) % 16
        z_copy(0, 0, z, frm).wait_recv()
        red[...] += taken(zrecv, pl.ds(frm, 1)).reshape(red.shape)
        return 0

    lax.fori_loop(0, 15, add, 0)
    move = pltpu.make_async_remote_copy(red, fin, f_ss.at[0], f_rs.at[0], device_id=home, device_id_type=MESH)
    move.start()
    move.wait()
    out_ref[...] = fin[...]

    halo_up.wait_send()
    halo_dn.wait_send()
    for copy in (s_copy, w_copy):
        for j in range(PARTS + PARTS // 2):
            for way in (0, 1):
                copy(way, j).wait_send()
    for g in range(4):
        combine(g).wait_send()

    def drain(w, s, d, o):
        @pl.when(o != 0)
        def _():
            z_copy(w, s, d, z).wait_send()

    for g in range(4):
        each(g, drain)


def on_device(snapshots, block_cols, mass_blocks):
    width = snapshots.shape[1]
    rows_b = block_cols.shape[0]
    snapshots = snapshots.reshape(rows_b, BLK, width)
    dma = pltpu.SemaphoreType.DMA
    steps = PARTS + PARTS // 2
    hbm = pl.BlockSpec(memory_space=pltpu.HBM)
    return pl.pallas_call(
        kernel,
        out_shape=jax.ShapeDtypeStruct((64, width), jnp.float32),
        in_specs=[hbm, hbm, hbm],
        out_specs=pl.BlockSpec(memory_space=pltpu.VMEM),
        scratch_shapes=[
            pltpu.SMEM(block_cols.shape[::-1], jnp.int32),
            pltpu.VMEM((rows_b + 2 * HB, BLK, width), jnp.bfloat16),
            pltpu.VMEM((4, rows_b, BLK, width), jnp.bfloat16),
            pltpu.VMEM((4, rows_b, BLK, width), jnp.bfloat16),
            pltpu.VMEM(mass_blocks.shape, jnp.bfloat16),
            pltpu.VMEM((4, 4, 2, 64, width), jnp.float32),
            pltpu.VMEM((4, 4, 64, width), jnp.float32),
            pltpu.VMEM((4, 4, 64, width), jnp.float32),
            pltpu.VMEM((4, 4, 40, width), jnp.int32),
            pltpu.VMEM((16, 40, width), jnp.int32),
            pltpu.VMEM((64, width), jnp.float32),
            pltpu.VMEM((64, width), jnp.float32),
            dma((3 + PARTS,)),
            dma((2,)), dma((2,)),
            dma((2, steps)), dma((2, steps)),
            dma((2, steps)), dma((2, steps)),
            dma((4,)), dma((4,)),
            dma((4, 4)), dma((16,)),
            dma((1,)), dma((1,)),
            pltpu.SemaphoreType.REGULAR((3,)),
        ],
        compiler_params=pltpu.CompilerParams(
            collective_id=0, has_side_effects=True, vmem_limit_bytes=60 * 2**20),
        name="gram",
    )(snapshots, block_cols.T, mass_blocks)


def solution(mesh):
    placed = (P("mesh", "run"), P("mesh", None), P("mesh", None, None))
    return jax.shard_map(
        on_device, mesh=mesh, in_specs=placed, out_specs=P("mesh", "run"), check_vma=False
    )
```

```python
import jax
import jax.numpy as jnp
from jax import lax
from jax.experimental import pallas as pl
from jax.experimental.pallas import tpu as pltpu
from jax.sharding import PartitionSpec as P

BLK = 64
HB = 2
MESH = pl.DeviceIdType.MESH
PARTS = 4


SENT = 33
CODE = 32000.0


def code(v):
    power = jnp.ceil(jnp.log2(jnp.maximum(jnp.max(jnp.abs(v), axis=1, keepdims=True), 1e-30)))
    q = jnp.round(v * (jnp.exp2(-power) * CODE)).astype(jnp.int32)
    half = v.shape[1] // 2
    return (q[:, :half] << 16) | (q[:, half:] & 0xFFFF), power.astype(jnp.int32)


def decode(pairs, power):
    q = jnp.concatenate([pairs >> 16, (pairs << 16) >> 16], axis=1)
    return q.astype(jnp.float32) * (jnp.exp2(power.astype(jnp.float32)) * (1 / CODE))


def kernel(
    snap_hbm, cols_hbm, mass_hbm, out_ref,
    cols, ext, sall, wall, mass, acc, comb, share, coded, zrecv, red, fin,
    load_sem, halo_ss, halo_rs, s_ss, s_rs, w_ss, w_rs, c_ss, c_rs, z_ss, z_rs, f_ss, f_rs, relay,
):
    m, r = lax.axis_index("mesh"), lax.axis_index("run")
    z, c, y, x = m // 2, m % 2, r // 4, r % 4
    kb, rows_b = cols.shape
    bpc = rows_b // PARTS

    def dev(z_, c_, y_, x_):
        return {"mesh": z_ * 2 + c_, "run": y_ * 4 + x_}

    y_up, y_dn = dev(z, c, (y + 1) % 4, x), dev(z, c, (y + 3) % 4, x)
    x_up, x_dn = dev(z, c, y, (x + 1) % 4), dev(z, c, y, (x + 3) % 4)
    m_up, m_dn = {"mesh": (m + 1) % 32, "run": r}, {"mesh": (m + 31) % 32, "run": r}
    sibling = dev(z, 1 - c, y, x)
    z_up, z_dn = dev((z + 1) % 16, c, y, x), dev((z + 15) % 16, c, y, x)
    over = (x + 2) % 4
    turn = (z % 4 + 4 - x) % 4
    back = jnp.where(turn == 1, 15, jnp.where(turn == 3, 1, 0))
    partner = dev((z + back) % 16, c, y, (x + jnp.where(turn == 1, 1, 3)) % 4)

    def greet(sem, devices):
        for d in devices:
            pl.semaphore_signal(sem, inc=1, device_id=d, device_id_type=MESH)

    barrier = pltpu.get_barrier_semaphore()
    greet(barrier, (y_up, y_dn, x_up, x_dn, m_up, m_dn, z_up, z_dn))

    load_ext = pltpu.make_async_copy(snap_hbm, ext.at[pl.ds(HB, rows_b)], load_sem.at[0])
    load_own = pltpu.make_async_copy(snap_hbm, sall.at[y], load_sem.at[1])
    load_ext.start()
    load_own.start()
    load_cols = pltpu.make_async_copy(cols_hbm, cols, load_sem.at[2])
    load_cols.start()
    order = (0, 3, 1, 2)
    loads = {}
    for j in order:
        part = pl.ds(j * bpc, bpc)
        loads[j] = pltpu.make_async_copy(mass_hbm.at[part], mass.at[part], load_sem.at[3 + j])
        loads[j].start()

    pl.semaphore_wait(barrier, 8)
    greet(relay.at[0], (z_up, z_dn, x_up, x_dn, sibling))

    def pass_on(i):
        pl.semaphore_wait(relay.at[i], (5, 2, 2, 1)[i])
        if i < 2:
            by = 2 ** (i + 1)
            greet(relay.at[i + 1], (dev((z + by) % 16, c, y, x), dev((z + 16 - by) % 16, c, y, x)))
        elif i == 2:
            greet(relay.at[3], (dev(z, c, y, over),))

    def part_of(way, j):
        return j % PARTS if way == 0 else PARTS - 1 - j % PARTS

    def ring(buf, ss, rs, pos, up, dn, way, j, incoming=False):
        back = 3 if way == 0 else 1
        far = (j // PARTS) + (1 if incoming else 0)
        slot = (pos + back * far) % 4
        rows = pl.ds(part_of(way, j) * bpc, bpc)
        return pltpu.make_async_remote_copy(
            buf.at[slot, rows], buf.at[slot, rows], ss.at[way, j], rs.at[way, j],
            device_id=up if way == 0 else dn, device_id_type=MESH,
        )

    def s_copy(way, j, incoming=False):
        return ring(sall, s_ss, s_rs, y, y_up, y_dn, way, j, incoming)

    def w_copy(way, j, incoming=False):
        return ring(wall, w_ss, w_rs, x, x_up, x_dn, way, j, incoming)

    load_ext.wait()
    halo_up = pltpu.make_async_remote_copy(
        ext.at[pl.ds(rows_b, HB)], ext.at[pl.ds(0, HB)], halo_ss.at[0], halo_rs.at[0],
        device_id=m_up, device_id_type=MESH)
    halo_dn = pltpu.make_async_remote_copy(
        ext.at[pl.ds(HB, HB)], ext.at[pl.ds(rows_b + HB, HB)], halo_ss.at[1], halo_rs.at[1],
        device_id=m_dn, device_id_type=MESH)
    halo_up.start()
    halo_dn.start()
    load_own.wait()
    half, whole, rest = range(PARTS // 2), range(PARTS // 2, PARTS), range(PARTS, PARTS + PARTS // 2)

    def begin(copy, steps):
        for j in steps:
            for way in (0, 1):
                copy(way, j).start()

    def left_here(copy, steps):
        for j in steps:
            for way in (0, 1):
                copy(way, j).wait_send()

    def arrived(copy, steps):
        for j in steps:
            for way in (0, 1):
                copy(way, j, True).wait_recv()

    begin(s_copy, half)

    halo_up.wait_recv()
    halo_dn.wait_recv()
    pass_on(0)
    load_cols.wait()
    base = m * rows_b - HB

    def weigh(b, _):
        picked = jnp.concatenate([ext[jnp.clip(cols[k, b] - base, 0, rows_b + 2 * HB - 1)] for k in range(kb)], axis=0)
        w = jnp.dot(mass[b], picked, preferred_element_type=jnp.float32)
        wall[x, b] = w.astype(jnp.bfloat16)
        return 0

    started = {0: 0, 1: 0}
    have = set()
    for j in order:
        loads[j].wait()
        lax.fori_loop(j * bpc, (j + 1) * bpc, weigh, 0, unroll=4)
        have.add(j)
        for way in (0, 1):
            while started[way] < PARTS // 2 and part_of(way, started[way]) in have:
                w_copy(way, started[way]).start()
                started[way] += 1

    begin(s_copy, whole)
    arrived(s_copy, half)
    begin(w_copy, whole)
    pass_on(1)
    left_here(s_copy, whole)
    begin(s_copy, rest)
    arrived(w_copy, half)

    def along_x(p):
        return p + p // 2 - 2 * (p // 3)

    def left(ps, j):
        rows = pl.ds(j * bpc, bpc)
        return jnp.concatenate([sall[(y + p + 3) % 4, rows].reshape(bpc * BLK, 128) for p in ps], axis=1)

    def right(ps, j):
        rows = pl.ds(j * bpc, bpc)
        return jnp.concatenate([wall[(x + along_x(p)) % 4, rows].reshape(bpc * BLK, 128) for p in ps], axis=1)

    def gram_part(ws, ss, j, first):
        d = lax.dot_general(left(ss, j), right(ws, j), (((0,), (0,)), ((), ())), preferred_element_type=jnp.float32)
        for iw, w in enumerate(ws):
            for i_s, s in enumerate(ss):
                t = d[128 * i_s:128 * (i_s + 1), 128 * iw:128 * (iw + 1)].reshape(2, 64, 128)
                if first:
                    acc[w, s] = t
                else:
                    acc[w, s] += t

    near, far = (0, 1, 2), (3,)
    three = pl.ds(0, 3)
    groups = (
        (3, lambda n: 0, lambda n: n, (0, three)),
        (3, lambda n: 1, lambda n: n, (1, three)),
        (3, lambda n: 2, lambda n: n, (2, three)),
        (3, lambda n: n, lambda n: 3, (three, 3)),
        (4, lambda n: 3, lambda n: (z // 4 + along_x(n) + 7 - y) % 4, (3, pl.ds(0, 4))),
    )

    def combine(g):
        w, s = groups[g][3]
        return pltpu.make_async_remote_copy(
            acc.at[w, s, 1 - c], comb.at[w, s], c_ss.at[g], c_rs.at[g], device_id=sibling, device_id_type=MESH)

    sent = pl.ds(0, SENT)

    def put(ref, v, *at):
        pairs, power = code(v.reshape(-1, *v.shape[-2:]))
        lead = v.shape[:-2]
        ref[*at, 0:32] = pairs.reshape(*lead, *pairs.shape[1:])
        ref[*at, 32:40] = jnp.broadcast_to(power, (power.shape[0], 8, power.shape[2])).reshape(*lead, 8, power.shape[2])

    def taken(ref, *at):
        pairs, power = ref[*at, 0:32], ref[*at, 32:33]
        lead = pairs.shape[:-2]
        v = decode(pairs.reshape(-1, *pairs.shape[-2:]), power.reshape(-1, *power.shape[-2:]))
        return v.reshape(*lead, *v.shape[1:])

    def z_copy(w, s, to, frm, column=x):
        return pltpu.make_async_remote_copy(
            coded.at[w, s, sent], zrecv.at[frm, sent], z_ss.at[w, s], z_rs.at[frm],
            device_id=dev(to, c, y, column), device_id_type=MESH)

    def chip(w, s):
        d = (((y + s + 3) % 4) * 4 + x + 16 + w % 3 - w % 3 // 2 * 3) % 16
        return d, (d - z + 16) % 16

    def each(g, body):
        def one(n, _):
            w, s = groups[g][1](n), groups[g][2](n)
            body(w, s, *chip(w, s))
            return 0

        lax.fori_loop(0, groups[g][0], one, 0)

    def send(g):
        at = groups[g][3]
        combine(g).wait_recv()
        share[*at] = acc[*at, c] + comb[*at]
        put(coded, share[*at], *at)

        def one(w, s, d, o):
            if g == 4:
                z_copy(w, s, d, z, over).start()
            else:
                @pl.when(o != 0)
                def _():
                    z_copy(w, s, d, z).start()

        each(g, one)

    def gram(ws, ss):
        for j in range(PARTS):
            gram_part(ws, ss, j, j == 0)

    arrived(s_copy, whole)
    gram((0,), near)
    combine(0).start()
    left_here(w_copy, whole)
    begin(w_copy, rest)
    pass_on(2)
    send(0)
    for way in (0, 1):
        for j in range(PARTS // 2, PARTS):
            w_copy(way, j, True).wait_recv()
        gram((2 - way,), near)
        combine(2 - way).start()
    send(2)
    send(1)
    arrived(s_copy, rest)
    gram(near, far)
    combine(3).start()
    pass_on(3)
    send(3)
    for j in range(PARTS, PARTS + PARTS // 2):
        for way in (0, 1):
            w_copy(way, j, True).wait_recv()
            gram_part(far, near + far, part_of(way, j), j == PARTS and way == 0)
    combine(4).start()
    send(4)

    @pl.when(turn == 2)
    def _():
        z_copy(0, 0, z, z).wait_recv()
        red[...] = taken(zrecv, pl.ds(z, 1)).reshape(red.shape)

    @pl.when(turn != 2)
    def _():
        red[...] = share[turn - turn // 3, ((z + back) % 16 // 4 - y + 5) % 4]

    def add(by, _):
        up, dn = (z + by) % 16, (z + 16 - by) % 16
        z_copy(0, 0, z, up).wait_recv()
        z_copy(0, 0, z, dn).wait_recv()
        red[...] += (taken(zrecv, pl.ds(up, 1)) + taken(zrecv, pl.ds(dn, 1))).reshape(red.shape)
        return 0

    lax.fori_loop(1, 8, add, 0)
    z_copy(0, 0, z, (z + 8) % 16).wait_recv()
    red[...] += taken(zrecv, pl.ds((z + 8) % 16, 1)).reshape(red.shape)

    @pl.when(turn % 2 == 1)
    def _():
        move = pltpu.make_async_remote_copy(
            red, fin, f_ss.at[0], f_rs.at[0], device_id=partner, device_id_type=MESH)
        move.start()
        move.wait()
        out_ref[...] = fin[...]

    @pl.when(turn % 2 == 0)
    def _():
        out_ref[...] = red[...]

    halo_up.wait_send()
    halo_dn.wait_send()
    for copy in (s_copy, w_copy):
        for steps in (half, rest):
            left_here(copy, steps)
    for g in range(5):
        combine(g).wait_send()

    def drain(w, s, d, o):
        @pl.when((o != 0) | (w == 3))
        def _():
            z_copy(w, s, d, z).wait_send()

    for g in range(5):
        each(g, drain)


def on_device(snapshots, block_cols, mass_blocks):
    width = snapshots.shape[1]
    rows_b = block_cols.shape[0]
    snapshots = snapshots.reshape(rows_b, BLK, width)
    dma = pltpu.SemaphoreType.DMA
    steps = PARTS + PARTS // 2
    hbm = pl.BlockSpec(memory_space=pltpu.HBM)
    return pl.pallas_call(
        kernel,
        out_shape=jax.ShapeDtypeStruct((64, width), jnp.float32),
        in_specs=[hbm, hbm, hbm],
        out_specs=pl.BlockSpec(memory_space=pltpu.VMEM),
        scratch_shapes=[
            pltpu.SMEM(block_cols.shape[::-1], jnp.int32),
            pltpu.VMEM((rows_b + 2 * HB, BLK, width), jnp.bfloat16),
            pltpu.VMEM((4, rows_b, BLK, width), jnp.bfloat16),
            pltpu.VMEM((4, rows_b, BLK, width), jnp.bfloat16),
            pltpu.VMEM(mass_blocks.shape, jnp.bfloat16),
            pltpu.VMEM((4, 4, 2, 64, width), jnp.float32),
            pltpu.VMEM((4, 4, 64, width), jnp.float32),
            pltpu.VMEM((4, 4, 64, width), jnp.float32),
            pltpu.VMEM((4, 4, 40, width), jnp.int32),
            pltpu.VMEM((16, 40, width), jnp.int32),
            pltpu.VMEM((64, width), jnp.float32),
            pltpu.VMEM((64, width), jnp.float32),
            dma((3 + PARTS,)),
            dma((2,)), dma((2,)),
            dma((2, steps)), dma((2, steps)),
            dma((2, steps)), dma((2, steps)),
            dma((5,)), dma((5,)),
            dma((4, 4)), dma((16,)),
            dma((1,)), dma((1,)),
            pltpu.SemaphoreType.REGULAR((4,)),
        ],
        compiler_params=pltpu.CompilerParams(
            collective_id=0, has_side_effects=True, vmem_limit_bytes=60 * 2**20),
        name="gram",
    )(snapshots, block_cols.T, mass_blocks)


def solution(mesh):
    placed = (P("mesh", "run"), P("mesh", None), P("mesh", None, None))
    return jax.shard_map(
        on_device, mesh=mesh, in_specs=placed, out_specs=P("mesh", "run"), check_vma=False
    )
```

```python
import jax
import jax.numpy as jnp
from jax import lax
from jax.experimental import pallas as pl
from jax.experimental.pallas import tpu as pltpu
from jax.sharding import PartitionSpec as P

BLK = 64
HB = 2
MESH = pl.DeviceIdType.MESH
PARTS = 4


SENT = 33
CODE = 32000.0


def code(v):
    power = jnp.ceil(jnp.log2(jnp.maximum(jnp.max(jnp.abs(v), axis=1, keepdims=True), 1e-30)))
    q = jnp.round(v * (jnp.exp2(-power) * CODE)).astype(jnp.int32)
    half = v.shape[1] // 2
    return (q[:, :half] << 16) | (q[:, half:] & 0xFFFF), power.astype(jnp.int32)


def decode(pairs, power):
    q = jnp.concatenate([pairs >> 16, (pairs << 16) >> 16], axis=1)
    return q.astype(jnp.float32) * (jnp.exp2(power.astype(jnp.float32)) * (1 / CODE))


def kernel(
    snap_hbm, cols_hbm, mass_hbm, out_ref,
    cols, ext, sall, wall, mass, acc, comb, share, coded, zrecv, red, fin,
    load_sem, halo_ss, halo_rs, s_ss, s_rs, w_ss, w_rs, c_ss, c_rs, z_ss, z_rs, f_ss, f_rs, relay,
):
    m, r = lax.axis_index("mesh"), lax.axis_index("run")
    z, c, y, x = m // 2, m % 2, r // 4, r % 4
    kb, rows_b = cols.shape
    bpc = rows_b // PARTS

    def dev(z_, c_, y_, x_):
        return {"mesh": z_ * 2 + c_, "run": y_ * 4 + x_}

    y_up, y_dn = dev(z, c, (y + 1) % 4, x), dev(z, c, (y + 3) % 4, x)
    x_up, x_dn = dev(z, c, y, (x + 1) % 4), dev(z, c, y, (x + 3) % 4)
    m_up, m_dn = {"mesh": (m + 1) % 32, "run": r}, {"mesh": (m + 31) % 32, "run": r}
    sibling = dev(z, 1 - c, y, x)
    z_up, z_dn = dev((z + 1) % 16, c, y, x), dev((z + 15) % 16, c, y, x)
    over = (x + 2) % 4
    turn = (z % 4 + 4 - x) % 4
    back = jnp.where(turn == 1, 15, jnp.where(turn == 3, 1, 0))
    partner = dev((z + back) % 16, c, y, (x + jnp.where(turn == 1, 1, 3)) % 4)

    def greet(sem, devices):
        for d in devices:
            pl.semaphore_signal(sem, inc=1, device_id=d, device_id_type=MESH)

    barrier = pltpu.get_barrier_semaphore()
    greet(barrier, (y_up, y_dn, x_up, x_dn, m_up, m_dn, z_up, z_dn))

    load_ext = pltpu.make_async_copy(snap_hbm, ext.at[pl.ds(HB, rows_b)], load_sem.at[0])
    load_own = pltpu.make_async_copy(snap_hbm, sall.at[y], load_sem.at[1])
    load_ext.start()
    load_own.start()
    load_cols = pltpu.make_async_copy(cols_hbm, cols, load_sem.at[2])
    load_cols.start()
    order = (0, 3, 1, 2)
    loads = {}
    for j in order:
        part = pl.ds(j * bpc, bpc)
        loads[j] = pltpu.make_async_copy(mass_hbm.at[part], mass.at[part], load_sem.at[3 + j])
        loads[j].start()

    pl.semaphore_wait(barrier, 8)
    greet(relay.at[0], (z_up, z_dn, x_up, x_dn, sibling))

    def pass_on(i):
        pl.semaphore_wait(relay.at[i], (5, 2, 2, 1)[i])
        if i < 2:
            by = 2 ** (i + 1)
            greet(relay.at[i + 1], (dev((z + by) % 16, c, y, x), dev((z + 16 - by) % 16, c, y, x)))
        elif i == 2:
            greet(relay.at[3], (dev(z, c, y, over),))

    def part_of(way, j):
        return j % PARTS if way == 0 else PARTS - 1 - j % PARTS

    def ring(buf, ss, rs, pos, up, dn, way, j, incoming=False):
        back = 3 if way == 0 else 1
        far = (j // PARTS) + (1 if incoming else 0)
        slot = (pos + back * far) % 4
        rows = pl.ds(part_of(way, j) * bpc, bpc)
        return pltpu.make_async_remote_copy(
            buf.at[slot, rows], buf.at[slot, rows], ss.at[way, j], rs.at[way, j],
            device_id=up if way == 0 else dn, device_id_type=MESH,
        )

    def s_copy(way, j, incoming=False):
        return ring(sall, s_ss, s_rs, y, y_up, y_dn, way, j, incoming)

    def w_copy(way, j, incoming=False):
        return ring(wall, w_ss, w_rs, x, x_up, x_dn, way, j, incoming)

    load_ext.wait()
    halo_up = pltpu.make_async_remote_copy(
        ext.at[pl.ds(rows_b, HB)], ext.at[pl.ds(0, HB)], halo_ss.at[0], halo_rs.at[0],
        device_id=m_up, device_id_type=MESH)
    halo_dn = pltpu.make_async_remote_copy(
        ext.at[pl.ds(HB, HB)], ext.at[pl.ds(rows_b + HB, HB)], halo_ss.at[1], halo_rs.at[1],
        device_id=m_dn, device_id_type=MESH)
    halo_up.start()
    halo_dn.start()
    load_own.wait()
    half, whole, rest = range(PARTS // 2), range(PARTS // 2, PARTS), range(PARTS, PARTS + PARTS // 2)

    def begin(copy, steps):
        for j in steps:
            for way in (0, 1):
                copy(way, j).start()

    def left_here(copy, steps):
        for j in steps:
            for way in (0, 1):
                copy(way, j).wait_send()

    def arrived(copy, steps):
        for j in steps:
            for way in (0, 1):
                copy(way, j, True).wait_recv()

    begin(s_copy, half)

    halo_up.wait_recv()
    halo_dn.wait_recv()
    pass_on(0)
    load_cols.wait()
    base = m * rows_b - HB

    def weigh(b, _):
        picked = jnp.concatenate([ext[jnp.clip(cols[k, b] - base, 0, rows_b + 2 * HB - 1)] for k in range(kb)], axis=0)
        w = jnp.dot(mass[b], picked, preferred_element_type=jnp.float32)
        wall[x, b] = w.astype(jnp.bfloat16)
        return 0

    started = {0: 0, 1: 0}
    have = set()
    for j in order:
        loads[j].wait()
        lax.fori_loop(j * bpc, (j + 1) * bpc, weigh, 0, unroll=8)
        have.add(j)
        for way in (0, 1):
            while started[way] < PARTS // 2 and part_of(way, started[way]) in have:
                w_copy(way, started[way]).start()
                started[way] += 1

    begin(w_copy, whole)
    begin(s_copy, whole)
    arrived(s_copy, half)
    pass_on(1)
    left_here(s_copy, whole)
    begin(s_copy, rest)
    arrived(w_copy, half)

    def along_x(p):
        return p + p // 2 - 2 * (p // 3)

    def left(ps, j):
        rows = pl.ds(j * bpc, bpc)
        return jnp.concatenate([sall[(y + p + 3) % 4, rows].reshape(bpc * BLK, 128) for p in ps], axis=1)

    def right(ps, j):
        rows = pl.ds(j * bpc, bpc)
        return jnp.concatenate([wall[(x + along_x(p)) % 4, rows].reshape(bpc * BLK, 128) for p in ps], axis=1)

    def gram_part(ws, ss, j, first):
        d = lax.dot_general(left(ss, j), right(ws, j), (((0,), (0,)), ((), ())), preferred_element_type=jnp.float32)
        for iw, w in enumerate(ws):
            for i_s, s in enumerate(ss):
                t = d[128 * i_s:128 * (i_s + 1), 128 * iw:128 * (iw + 1)].reshape(2, 64, 128)
                if first:
                    acc[w, s] = t
                else:
                    acc[w, s] += t

    near, far = (0, 1, 2), (3,)
    three = pl.ds(0, 3)
    groups = (
        (3, lambda n: 0, lambda n: n, (0, three)),
        (3, lambda n: 1, lambda n: n, (1, three)),
        (3, lambda n: 2, lambda n: n, (2, three)),
        (3, lambda n: n, lambda n: 3, (three, 3)),
        (4, lambda n: 3, lambda n: (z // 4 + along_x(n) + 7 - y) % 4, (3, pl.ds(0, 4))),
    )

    def combine(g):
        w, s = groups[g][3]
        return pltpu.make_async_remote_copy(
            acc.at[w, s, 1 - c], comb.at[w, s], c_ss.at[g], c_rs.at[g], device_id=sibling, device_id_type=MESH)

    sent = pl.ds(0, SENT)

    def put(ref, v, *at):
        pairs, power = code(v.reshape(-1, *v.shape[-2:]))
        lead = v.shape[:-2]
        ref[*at, 0:32] = pairs.reshape(*lead, *pairs.shape[1:])
        ref[*at, 32:40] = jnp.broadcast_to(power, (power.shape[0], 8, power.shape[2])).reshape(*lead, 8, power.shape[2])

    def taken(ref, *at):
        pairs, power = ref[*at, 0:32], ref[*at, 32:33]
        lead = pairs.shape[:-2]
        v = decode(pairs.reshape(-1, *pairs.shape[-2:]), power.reshape(-1, *power.shape[-2:]))
        return v.reshape(*lead, *v.shape[1:])

    def z_copy(w, s, to, frm, column=x):
        return pltpu.make_async_remote_copy(
            coded.at[w, s, sent], zrecv.at[frm, sent], z_ss.at[w, s], z_rs.at[frm],
            device_id=dev(to, c, y, column), device_id_type=MESH)

    def chip(w, s):
        d = (((y + s + 3) % 4) * 4 + x + 16 + w % 3 - w % 3 // 2 * 3) % 16
        return d, (d - z + 16) % 16

    def each(g, body):
        def one(n, _):
            w, s = groups[g][1](n), groups[g][2](n)
            body(w, s, *chip(w, s))
            return 0

        lax.fori_loop(0, groups[g][0], one, 0)

    def send(g):
        at = groups[g][3]
        combine(g).wait_recv()
        share[*at] = acc[*at, c] + comb[*at]
        put(coded, share[*at], *at)

        def one(w, s, d, o):
            if g == 4:
                z_copy(w, s, d, z, over).start()
            else:
                @pl.when(o != 0)
                def _():
                    z_copy(w, s, d, z).start()

        each(g, one)

    def gram(ws, ss):
        for j in range(PARTS):
            gram_part(ws, ss, j, j == 0)

    arrived(s_copy, whole)
    gram((0,), near)
    combine(0).start()
    left_here(w_copy, whole)
    begin(w_copy, rest)
    pass_on(2)
    send(0)
    for way in (0, 1):
        for j in range(PARTS // 2, PARTS):
            w_copy(way, j, True).wait_recv()
        gram((2 - way,), near)
        combine(2 - way).start()
    send(2)
    send(1)
    arrived(s_copy, rest)
    gram(near, far)
    combine(3).start()
    pass_on(3)
    send(3)
    for j in range(PARTS, PARTS + PARTS // 2):
        for way in (0, 1):
            w_copy(way, j, True).wait_recv()
            gram_part(far, near + far, part_of(way, j), j == PARTS and way == 0)
    combine(4).start()
    send(4)

    @pl.when(turn == 2)
    def _():
        z_copy(0, 0, z, z).wait_recv()
        red[...] = taken(zrecv, pl.ds(z, 1)).reshape(red.shape)

    @pl.when(turn != 2)
    def _():
        red[...] = share[turn - turn // 3, ((z + back) % 16 // 4 - y + 5) % 4]

    def add(by, _):
        up, dn = (z + by) % 16, (z + 16 - by) % 16
        z_copy(0, 0, z, up).wait_recv()
        z_copy(0, 0, z, dn).wait_recv()
        red[...] += (taken(zrecv, pl.ds(up, 1)) + taken(zrecv, pl.ds(dn, 1))).reshape(red.shape)
        return 0

    lax.fori_loop(1, 8, add, 0)
    z_copy(0, 0, z, (z + 8) % 16).wait_recv()
    red[...] += taken(zrecv, pl.ds((z + 8) % 16, 1)).reshape(red.shape)

    @pl.when(turn % 2 == 1)
    def _():
        move = pltpu.make_async_remote_copy(
            red, fin, f_ss.at[0], f_rs.at[0], device_id=partner, device_id_type=MESH)
        move.start()
        move.wait()
        out_ref[...] = fin[...]

    @pl.when(turn % 2 == 0)
    def _():
        out_ref[...] = red[...]

    halo_up.wait_send()
    halo_dn.wait_send()
    for copy in (s_copy, w_copy):
        for steps in (half, rest):
            left_here(copy, steps)
    for g in range(5):
        combine(g).wait_send()

    def drain(w, s, d, o):
        @pl.when((o != 0) | (w == 3))
        def _():
            z_copy(w, s, d, z).wait_send()

    for g in range(5):
        each(g, drain)


def on_device(snapshots, block_cols, mass_blocks):
    width = snapshots.shape[1]
    rows_b = block_cols.shape[0]
    snapshots = snapshots.reshape(rows_b, BLK, width)
    dma = pltpu.SemaphoreType.DMA
    steps = PARTS + PARTS // 2
    hbm = pl.BlockSpec(memory_space=pltpu.HBM)
    return pl.pallas_call(
        kernel,
        out_shape=jax.ShapeDtypeStruct((64, width), jnp.float32),
        in_specs=[hbm, hbm, hbm],
        out_specs=pl.BlockSpec(memory_space=pltpu.VMEM),
        scratch_shapes=[
            pltpu.SMEM(block_cols.shape[::-1], jnp.int32),
            pltpu.VMEM((rows_b + 2 * HB, BLK, width), jnp.bfloat16),
            pltpu.VMEM((4, rows_b, BLK, width), jnp.bfloat16),
            pltpu.VMEM((4, rows_b, BLK, width), jnp.bfloat16),
            pltpu.VMEM(mass_blocks.shape, jnp.bfloat16),
            pltpu.VMEM((4, 4, 2, 64, width), jnp.float32),
            pltpu.VMEM((4, 4, 64, width), jnp.float32),
            pltpu.VMEM((4, 4, 64, width), jnp.float32),
            pltpu.VMEM((4, 4, 40, width), jnp.int32),
            pltpu.VMEM((16, 40, width), jnp.int32),
            pltpu.VMEM((64, width), jnp.float32),
            pltpu.VMEM((64, width), jnp.float32),
            dma((3 + PARTS,)),
            dma((2,)), dma((2,)),
            dma((2, steps)), dma((2, steps)),
            dma((2, steps)), dma((2, steps)),
            dma((5,)), dma((5,)),
            dma((4, 4)), dma((16,)),
            dma((1,)), dma((1,)),
            pltpu.SemaphoreType.REGULAR((4,)),
        ],
        compiler_params=pltpu.CompilerParams(
            collective_id=0, has_side_effects=True, vmem_limit_bytes=60 * 2**20),
        name="gram",
    )(snapshots, block_cols.T, mass_blocks)


def solution(mesh):
    placed = (P("mesh", "run"), P("mesh", None), P("mesh", None, None))
    return jax.shard_map(
        on_device, mesh=mesh, in_specs=placed, out_specs=P("mesh", "run"), check_vma=False
    )
```

```python
import jax
import jax.numpy as jnp
from jax import lax
from jax.experimental import pallas as pl
from jax.experimental.pallas import tpu as pltpu
from jax.sharding import PartitionSpec as P

BLK = 64
HB = 2
MESH = pl.DeviceIdType.MESH
PARTS = 4


SENT = 33
CODE = 32000.0


def code(v):
    power = jnp.ceil(jnp.log2(jnp.maximum(jnp.max(jnp.abs(v), axis=1, keepdims=True), 1e-30)))
    q = jnp.round(v * (jnp.exp2(-power) * CODE)).astype(jnp.int32)
    half = v.shape[1] // 2
    return (q[:, :half] << 16) | (q[:, half:] & 0xFFFF), power.astype(jnp.int32)


def decode(pairs, power):
    q = jnp.concatenate([pairs >> 16, (pairs << 16) >> 16], axis=1)
    return q.astype(jnp.float32) * (jnp.exp2(power.astype(jnp.float32)) * (1 / CODE))


def kernel(
    snap_hbm, cols_hbm, mass_hbm, out_ref,
    cols, ext, sall, wall, mass, acc, comb, share, coded, zrecv, red, fin,
    load_sem, halo_ss, halo_rs, s_ss, s_rs, w_ss, w_rs, c_ss, c_rs, z_ss, z_rs, f_ss, f_rs, relay,
):
    m, r = lax.axis_index("mesh"), lax.axis_index("run")
    z, c, y, x = m // 2, m % 2, r // 4, r % 4
    kb, rows_b = cols.shape
    bpc = rows_b // PARTS

    def dev(z_, c_, y_, x_):
        return {"mesh": z_ * 2 + c_, "run": y_ * 4 + x_}

    y_up, y_dn = dev(z, c, (y + 1) % 4, x), dev(z, c, (y + 3) % 4, x)
    x_up, x_dn = dev(z, c, y, (x + 1) % 4), dev(z, c, y, (x + 3) % 4)
    m_up, m_dn = {"mesh": (m + 1) % 32, "run": r}, {"mesh": (m + 31) % 32, "run": r}
    sibling = dev(z, 1 - c, y, x)
    z_up, z_dn = dev((z + 1) % 16, c, y, x), dev((z + 15) % 16, c, y, x)
    over = (x + 2) % 4
    turn = (z % 4 + 4 - x) % 4
    back = jnp.where(turn == 1, 15, jnp.where(turn == 3, 1, 0))
    partner = dev((z + back) % 16, c, y, (x + jnp.where(turn == 1, 1, 3)) % 4)

    def greet(sem, devices):
        for d in devices:
            pl.semaphore_signal(sem, inc=1, device_id=d, device_id_type=MESH)

    barrier = pltpu.get_barrier_semaphore()
    greet(barrier, (y_up, y_dn, x_up, x_dn, m_up, m_dn, z_up, z_dn))

    load_ext = pltpu.make_async_copy(snap_hbm, ext.at[pl.ds(HB, rows_b)], load_sem.at[0])
    load_own = pltpu.make_async_copy(snap_hbm, sall.at[y], load_sem.at[1])
    load_ext.start()
    load_own.start()
    load_cols = pltpu.make_async_copy(cols_hbm, cols, load_sem.at[2])
    load_cols.start()
    order = (0, 3, 1, 2)
    loads = {}
    for j in order:
        part = pl.ds(j * bpc, bpc)
        loads[j] = pltpu.make_async_copy(mass_hbm.at[part], mass.at[part], load_sem.at[3 + j])
        loads[j].start()

    pl.semaphore_wait(barrier, 8)
    greet(relay.at[0], (z_up, z_dn, x_up, x_dn, sibling))

    def pass_on(i):
        pl.semaphore_wait(relay.at[i], (5, 2, 2, 1)[i])
        if i < 2:
            by = 2 ** (i + 1)
            greet(relay.at[i + 1], (dev((z + by) % 16, c, y, x), dev((z + 16 - by) % 16, c, y, x)))
        elif i == 2:
            greet(relay.at[3], (dev(z, c, y, over),))

    def part_of(way, j):
        return j % PARTS if way == 0 else PARTS - 1 - j % PARTS

    def ring(buf, ss, rs, pos, up, dn, way, j, incoming=False):
        back = 3 if way == 0 else 1
        far = (j // PARTS) + (1 if incoming else 0)
        slot = (pos + back * far) % 4
        rows = pl.ds(part_of(way, j) * bpc, bpc)
        return pltpu.make_async_remote_copy(
            buf.at[slot, rows], buf.at[slot, rows], ss.at[way, j], rs.at[way, j],
            device_id=up if way == 0 else dn, device_id_type=MESH,
        )

    def s_copy(way, j, incoming=False):
        return ring(sall, s_ss, s_rs, y, y_up, y_dn, way, j, incoming)

    def w_copy(way, j, incoming=False):
        return ring(wall, w_ss, w_rs, x, x_up, x_dn, way, j, incoming)

    load_ext.wait()
    halo_up = pltpu.make_async_remote_copy(
        ext.at[pl.ds(rows_b, HB)], ext.at[pl.ds(0, HB)], halo_ss.at[0], halo_rs.at[0],
        device_id=m_up, device_id_type=MESH)
    halo_dn = pltpu.make_async_remote_copy(
        ext.at[pl.ds(HB, HB)], ext.at[pl.ds(rows_b + HB, HB)], halo_ss.at[1], halo_rs.at[1],
        device_id=m_dn, device_id_type=MESH)
    halo_up.start()
    halo_dn.start()
    load_own.wait()
    half, whole, rest = range(PARTS // 2), range(PARTS // 2, PARTS), range(PARTS, PARTS + PARTS // 2)

    def begin(copy, steps):
        for j in steps:
            for way in (0, 1):
                copy(way, j).start()

    def left_here(copy, steps):
        for j in steps:
            for way in (0, 1):
                copy(way, j).wait_send()

    def arrived(copy, steps):
        for j in steps:
            for way in (0, 1):
                copy(way, j, True).wait_recv()

    begin(s_copy, half)

    halo_up.wait_recv()
    halo_dn.wait_recv()
    pass_on(0)
    load_cols.wait()
    base = m * rows_b - HB

    def weigh(b, _):
        picked = jnp.concatenate([ext[jnp.clip(cols[k, b] - base, 0, rows_b + 2 * HB - 1)] for k in range(kb)], axis=0)
        w = jnp.dot(mass[b], picked, preferred_element_type=jnp.float32)
        wall[x, b] = w.astype(jnp.bfloat16)
        return 0

    started = {0: 0, 1: 0}
    have = set()
    for j in order:
        loads[j].wait()
        lax.fori_loop(j * bpc, (j + 1) * bpc, weigh, 0, unroll=8)
        have.add(j)
        for way in (0, 1):
            while started[way] < PARTS // 2 and part_of(way, started[way]) in have:
                w_copy(way, started[way]).start()
                started[way] += 1

    begin(w_copy, whole)
    begin(s_copy, whole)
    arrived(s_copy, half)
    pass_on(1)
    left_here(s_copy, whole)
    begin(s_copy, rest)
    arrived(w_copy, half)

    def along_x(p):
        return p + p // 2 - 2 * (p // 3)

    def left(ps, j):
        rows = pl.ds(j * bpc, bpc)
        return jnp.concatenate([sall[(y + p + 3) % 4, rows].reshape(bpc * BLK, 128) for p in ps], axis=1)

    def right(ps, j):
        rows = pl.ds(j * bpc, bpc)
        return jnp.concatenate([wall[(x + along_x(p)) % 4, rows].reshape(bpc * BLK, 128) for p in ps], axis=1)

    def gram_part(ws, ss, j, first):
        d = lax.dot_general(left(ss, j), right(ws, j), (((0,), (0,)), ((), ())), preferred_element_type=jnp.float32)
        for iw, w in enumerate(ws):
            for i_s, s in enumerate(ss):
                t = d[128 * i_s:128 * (i_s + 1), 128 * iw:128 * (iw + 1)].reshape(2, 64, 128)
                if first:
                    acc[w, s] = t
                else:
                    acc[w, s] += t

    near, far = (0, 1, 2), (3,)
    three = pl.ds(0, 3)
    groups = (
        (3, lambda n: 0, lambda n: n, (0, three)),
        (3, lambda n: 1, lambda n: n, (1, three)),
        (3, lambda n: 2, lambda n: n, (2, three)),
        (3, lambda n: n, lambda n: 3, (three, 3)),
        (2, lambda n: 3, lambda n: n, (3, pl.ds(0, 2))),
        (2, lambda n: 3, lambda n: 2 + n, (3, pl.ds(2, 2))),
    )

    def combine(g):
        w, s = groups[g][3]
        return pltpu.make_async_remote_copy(
            acc.at[w, s, 1 - c], comb.at[w, s], c_ss.at[g], c_rs.at[g], device_id=sibling, device_id_type=MESH)

    sent = pl.ds(0, SENT)

    def put(ref, v, *at):
        pairs, power = code(v.reshape(-1, *v.shape[-2:]))
        lead = v.shape[:-2]
        ref[*at, 0:32] = pairs.reshape(*lead, *pairs.shape[1:])
        ref[*at, 32:40] = jnp.broadcast_to(power, (power.shape[0], 8, power.shape[2])).reshape(*lead, 8, power.shape[2])

    def taken(ref, *at):
        pairs, power = ref[*at, 0:32], ref[*at, 32:33]
        lead = pairs.shape[:-2]
        v = decode(pairs.reshape(-1, *pairs.shape[-2:]), power.reshape(-1, *power.shape[-2:]))
        return v.reshape(*lead, *v.shape[1:])

    def z_copy(w, s, to, frm, column=x):
        return pltpu.make_async_remote_copy(
            coded.at[w, s, sent], zrecv.at[frm, sent], z_ss.at[w, s], z_rs.at[frm],
            device_id=dev(to, c, y, column), device_id_type=MESH)

    def chip(w, s):
        d = (((y + s + 3) % 4) * 4 + x + 16 + w % 3 - w % 3 // 2 * 3) % 16
        return d, (d - z + 16) % 16

    def each(g, body):
        def one(n, _):
            w, s = groups[g][1](n), groups[g][2](n)
            body(w, s, *chip(w, s))
            return 0

        lax.fori_loop(0, groups[g][0], one, 0, unroll=True)

    def send(g):
        at = groups[g][3]
        combine(g).wait_recv()
        share[*at] = acc[*at, c] + comb[*at]
        put(coded, share[*at], *at)

        def one(w, s, d, o):
            if g >= 4:
                z_copy(w, s, d, z, over).start()
            else:
                @pl.when(o != 0)
                def _():
                    z_copy(w, s, d, z).start()

        each(g, one)

    def gram(ws, ss):
        for j in range(PARTS):
            gram_part(ws, ss, j, j == 0)

    arrived(s_copy, whole)
    gram((0,), near)
    combine(0).start()
    left_here(w_copy, whole)
    begin(w_copy, rest)
    pass_on(2)
    send(0)
    for way in (0, 1):
        for j in range(PARTS // 2, PARTS):
            w_copy(way, j, True).wait_recv()
        gram((2 - way,), near)
        combine(2 - way).start()
    send(2)
    send(1)
    arrived(s_copy, rest)
    gram(near, far)
    combine(3).start()
    pass_on(3)
    send(3)
    for j in rest:
        last = j == rest[-1]
        for way in (0, 1):
            w_copy(way, j, True).wait_recv()
            if not last:
                gram_part(far, near + far, part_of(way, j), j == PARTS and way == 0)
    for g, ss in ((4, (0, 1)), (5, (2, 3))):
        for way in (0, 1):
            gram_part(far, ss, part_of(way, rest[-1]), False)
        combine(g).start()
    send(4)
    send(5)

    @pl.when(turn == 2)
    def _():
        z_copy(0, 0, z, z).wait_recv()
        red[...] = taken(zrecv, pl.ds(z, 1)).reshape(red.shape)

    @pl.when(turn != 2)
    def _():
        red[...] = share[turn - turn // 3, ((z + back) % 16 // 4 - y + 5) % 4]

    def add(by, _):
        up, dn = (z + by) % 16, (z + 16 - by) % 16
        z_copy(0, 0, z, up).wait_recv()
        z_copy(0, 0, z, dn).wait_recv()
        red[...] += (taken(zrecv, pl.ds(up, 1)) + taken(zrecv, pl.ds(dn, 1))).reshape(red.shape)
        return 0

    lax.fori_loop(1, 8, add, 0)
    z_copy(0, 0, z, (z + 8) % 16).wait_recv()
    red[...] += taken(zrecv, pl.ds((z + 8) % 16, 1)).reshape(red.shape)

    @pl.when(turn % 2 == 1)
    def _():
        move = pltpu.make_async_remote_copy(
            red, fin, f_ss.at[0], f_rs.at[0], device_id=partner, device_id_type=MESH)
        move.start()
        move.wait()
        out_ref[...] = fin[...]

    @pl.when(turn % 2 == 0)
    def _():
        out_ref[...] = red[...]

    halo_up.wait_send()
    halo_dn.wait_send()
    for copy in (s_copy, w_copy):
        for steps in (half, rest):
            left_here(copy, steps)
    for g in range(6):
        combine(g).wait_send()

    def drain(w, s, d, o):
        @pl.when((o != 0) | (w == 3))
        def _():
            z_copy(w, s, d, z).wait_send()

    for g in range(6):
        each(g, drain)


def on_device(snapshots, block_cols, mass_blocks):
    width = snapshots.shape[1]
    rows_b = block_cols.shape[0]
    snapshots = snapshots.reshape(rows_b, BLK, width)
    dma = pltpu.SemaphoreType.DMA
    steps = PARTS + PARTS // 2
    hbm = pl.BlockSpec(memory_space=pltpu.HBM)
    return pl.pallas_call(
        kernel,
        out_shape=jax.ShapeDtypeStruct((64, width), jnp.float32),
        in_specs=[hbm, hbm, hbm],
        out_specs=pl.BlockSpec(memory_space=pltpu.VMEM),
        scratch_shapes=[
            pltpu.SMEM(block_cols.shape[::-1], jnp.int32),
            pltpu.VMEM((rows_b + 2 * HB, BLK, width), jnp.bfloat16),
            pltpu.VMEM((4, rows_b, BLK, width), jnp.bfloat16),
            pltpu.VMEM((4, rows_b, BLK, width), jnp.bfloat16),
            pltpu.VMEM(mass_blocks.shape, jnp.bfloat16),
            pltpu.VMEM((4, 4, 2, 64, width), jnp.float32),
            pltpu.VMEM((4, 4, 64, width), jnp.float32),
            pltpu.VMEM((4, 4, 64, width), jnp.float32),
            pltpu.VMEM((4, 4, 40, width), jnp.int32),
            pltpu.VMEM((16, 40, width), jnp.int32),
            pltpu.VMEM((64, width), jnp.float32),
            pltpu.VMEM((64, width), jnp.float32),
            dma((3 + PARTS,)),
            dma((2,)), dma((2,)),
            dma((2, steps)), dma((2, steps)),
            dma((2, steps)), dma((2, steps)),
            dma((6,)), dma((6,)),
            dma((4, 4)), dma((16,)),
            dma((1,)), dma((1,)),
            pltpu.SemaphoreType.REGULAR((4,)),
        ],
        compiler_params=pltpu.CompilerParams(
            collective_id=0, has_side_effects=True, vmem_limit_bytes=60 * 2**20),
        name="gram",
    )(snapshots, block_cols.T, mass_blocks)


def solution(mesh):
    placed = (P("mesh", "run"), P("mesh", None), P("mesh", None, None))
    return jax.shard_map(
        on_device, mesh=mesh, in_specs=placed, out_specs=P("mesh", "run"), check_vma=False
    )
```
